256 devices in a mesh: seq: 8 (over z), sub: 32 (over y, x, core).
Axes of the slice: x: 4, y: 4, z: 8, core: 2. Of those that a mesh axis runs over, the one named last changes fastest.
Arguments:
- queries: bfloat16 [65536, 512], P(('seq', 'sub')), may hold values from -7 to 7
- keys: bfloat16 [65536, 512], P(('seq', 'sub')), may hold values from -7 to 7
- values: bfloat16 [65536, 512], P(('seq', 'sub')), may hold values from -7 to 7
- cotangent: bfloat16 [65536, 512], P(('seq', 'sub')), may hold values from -6 to 6
Outputs:
- attention: bfloat16 [65536, 512], P(('seq', 'sub'))
- query_grad: bfloat16 [65536, 512], P(('seq', 'sub'))
- key_grad: bfloat16 [65536, 512], P(('seq', 'sub'))
- value_grad: bfloat16 [65536, 512], P(('seq', 'sub'))
The draws below stay inside these ranges and needn't reach their ends.
All inputs are finite; a program needn't handle non-finite values.
Results may differ from the reference program's by a relative error of at most 0.01.
Values may be sent and summed in bfloat16 or wider, within the bound.
A program may use at most 128 MiB of HBM per device.

```python
import math
import jax
import jax.numpy as jnp
from jax import lax

HEADS = 8
HEAD = 64
BLOCK = 256
LEVELS = 4
D = 512
SEQ = 65536


def layered_offsets(key):
    positions = jnp.arange(SEQ)
    summed = jnp.zeros((SEQ, HEADS * HEAD), jnp.float32)
    for section_index in range(LEVELS):
        stride = BLOCK * 2 ** section_index // 2
        offsets = 0.5 * jax.random.normal(jax.random.fold_in(key, section_index), (SEQ // stride, HEADS * HEAD), jnp.float32)
        summed = summed + offsets[positions // stride]
    return summed


def draw_queries(key, part):
    key = jax.random.fold_in(key, 17)
    noise_part = jax.random.normal(key, (SEQ, HEADS * HEAD), jnp.float32)
    return jnp.clip(noise_part, -7.0, 7.0).astype(jnp.bfloat16)


def draw_keys(key, part):
    key = jax.random.fold_in(key, 11)
    noise_part = jax.random.normal(key, (SEQ, HEADS * HEAD), jnp.float32)
    mixed = 0.8 * (noise_part + layered_offsets(jax.random.fold_in(key, 1)))
    return jnp.clip(mixed, -7.0, 7.0).astype(jnp.bfloat16)


def draw_values(key, part):
    key = jax.random.fold_in(key, 13)
    noise_part = jax.random.normal(key, (SEQ, HEADS * HEAD), jnp.float32)
    mixed = 0.8 * (noise_part + layered_offsets(jax.random.fold_in(key, 1)))
    return jnp.clip(mixed, -7.0, 7.0).astype(jnp.bfloat16)


def level_of(rng, shape, cuts, low, high):
    def one(axis_at, parts):
        steps = jax.random.uniform(jax.random.fold_in(jax.random.fold_in(rng, 6), axis_at), (parts,), jnp.float32, low / len(cuts), high / len(cuts))
        return jnp.repeat(jnp.exp(steps), shape[axis_at] // parts).reshape((-1,) + (1,) * (len(shape) - axis_at - 1))

    gain = one(*cuts[0])
    for cut in cuts[1:]:
        gain = gain * one(*cut)
    return gain


def centred(stream_key, extent, scale, most, split=(), held_as=jnp.bfloat16):
    factor_of = level_of(stream_key, extent, split, -0.22, 0.18) if split else 1.0
    array = jax.random.normal(stream_key, extent, jnp.float32) * scale * factor_of
    return jnp.minimum(jnp.maximum(array, -most), most).astype(held_as)


def setup_inputs(seed: int = 0) -> dict:
    splits = jax.random.split(jax.random.key(seed), 5)
    queries = draw_queries(jax.random.fold_in(splits[4], 71), 0)
    keys = draw_keys(jax.random.fold_in(splits[4], 71), 0)
    values = draw_values(jax.random.fold_in(splits[4], 71), 0)
    cotangent = centred(splits[3], (SEQ, D), 1.0, 6.0, ((0, 256),))
    return {"queries": queries, "keys": keys, "values": values, "cotangent": cotangent}


masked_score = -1e+30

def coarsen(stacked):
    paired = stacked.astype(jnp.float32).reshape(stacked.shape[0], stacked.shape[1] // 2, 2, stacked.shape[2])
    return (0.5 * (paired[:, :, 0] + paired[:, :, 1])).astype(jnp.bfloat16)

def reference(queries, keys, values, cotangent):
    block_count = SEQ // BLOCK
    levels = min(LEVELS, block_count.bit_length() - 2)
    half_rows = BLOCK // 2
    feature_count = HEADS * HEAD
    score_scale = 1.0 / math.sqrt(HEAD)
    pyramid = [jnp.stack([keys, values])]
    for level_index in range(1, levels + 1):
        pyramid.append(coarsen(pyramid[-1]))
    padded = [jnp.pad(pyramid[0], ((0, 0), (BLOCK, BLOCK), (0, 0)))]
    for level_index in range(1, levels + 1):
        padded.append(jnp.pad(pyramid[level_index], ((0, 0), (3 * half_rows, 3 * half_rows), (0, 0))))
    grad_start = tuple((jnp.zeros(item.shape, jnp.float32) for item in padded))

    def one_block(grad_carry, block_index):
        start_row = (block_index * BLOCK).astype(jnp.int32)
        locations = [(0, start_row, 3 * BLOCK)]
        pieces = [lax.dynamic_slice_in_dim(padded[0], start_row, 3 * BLOCK, 1)]
        near_flags = jnp.stack([block_index >= 1, block_index >= 0, block_index < block_count - 1])
        validity = [jnp.repeat(near_flags, BLOCK)]
        for level_index in range(1, levels + 1):
            halves = pyramid[level_index].shape[1] // half_rows
            group_index = block_index // 2 ** (level_index - 1)
            third_group = jnp.where(group_index % 2 == 0, group_index + 3, group_index - 3)
            for target in (group_index - 2, group_index + 2, third_group):
                piece_start = ((target + 3) * half_rows).astype(jnp.int32)
                locations.append((level_index, piece_start, half_rows))
                pieces.append(lax.dynamic_slice_in_dim(padded[level_index], piece_start, half_rows, 1))
                inside = jnp.logical_and(target >= 0, target < halves)
                validity.append(jnp.repeat(inside[None], half_rows))
        key_all = jnp.concatenate(pieces, axis=1)
        valid_all = jnp.concatenate(validity)
        key_count = key_all.shape[1]
        key_block = key_all[0].astype(jnp.float32).reshape(key_count, HEADS, HEAD)
        value_block = key_all[1].astype(jnp.float32).reshape(key_count, HEADS, HEAD)
        query_block = lax.dynamic_slice_in_dim(queries, start_row, BLOCK, 0).astype(jnp.float32).reshape(BLOCK, HEADS, HEAD)
        cotangent_block = lax.dynamic_slice_in_dim(cotangent, start_row, BLOCK, 0).astype(jnp.float32).reshape(BLOCK, HEADS, HEAD)
        scores = jnp.einsum('qhe,khe->hqk', query_block, key_block) * score_scale
        scores = jnp.where(valid_all[None, None, :], scores, masked_score)
        row_top = lax.optimization_barrier(jnp.max(scores, axis=2, keepdims=True))
        weight = jnp.exp(scores - row_top)
        total_weight = lax.optimization_barrier(jnp.sum(weight, axis=2, keepdims=True))
        rounded_weight = lax.optimization_barrier(weight.astype(jnp.bfloat16)).astype(jnp.float32)
        attended = jnp.einsum('hqk,khe->qhe', rounded_weight, value_block) / jnp.transpose(total_weight, (1, 0, 2))
        probability = weight / total_weight
        prob_grad = jnp.einsum('qhe,khe->hqk', cotangent_block, value_block)
        delta_term = jnp.transpose(lax.optimization_barrier(jnp.sum(cotangent_block * attended, axis=2, keepdims=True)), (1, 0, 2))
        dscore = lax.optimization_barrier((probability * (prob_grad - delta_term)).astype(jnp.bfloat16)).astype(jnp.float32)
        rounded_prob = lax.optimization_barrier(probability.astype(jnp.bfloat16)).astype(jnp.float32)
        query_part = jnp.einsum('hqk,khe->qhe', dscore, key_block) * score_scale
        key_part = jnp.einsum('hqk,qhe->khe', dscore, query_block) * score_scale
        value_part = jnp.einsum('hqk,qhe->khe', rounded_prob, cotangent_block)
        grads = jnp.stack([key_part.reshape(key_count, feature_count), value_part.reshape(key_count, feature_count)])
        new_carry = list(grad_carry)
        offset = 0
        for level_index, piece_start, length in locations:
            segment = grads[:, offset:offset + length]
            current = lax.dynamic_slice_in_dim(new_carry[level_index], piece_start, length, 1)
            new_carry[level_index] = lax.dynamic_update_slice_in_dim(new_carry[level_index], current + segment, piece_start, 1)
            offset += length
        outputs = (attended.reshape(BLOCK, feature_count).astype(jnp.bfloat16), query_part.reshape(BLOCK, feature_count).astype(jnp.bfloat16))
        return (tuple(new_carry), outputs)
    grad_final, outputs = lax.scan(one_block, grad_start, jnp.arange(block_count, dtype=jnp.int32))
    attention = outputs[0].reshape(SEQ, feature_count)
    query_grad = outputs[1].reshape(SEQ, feature_count)
    level_grads = [grad_final[0][:, BLOCK:-BLOCK]]
    for level_index in range(1, levels + 1):
        level_grads.append(grad_final[level_index][:, 3 * half_rows:-3 * half_rows])
    running = level_grads[levels]
    for level_index in range(levels, 0, -1):
        running = level_grads[level_index - 1] + 0.5 * jnp.repeat(running, 2, axis=1)
    return (attention, query_grad, running[0].astype(jnp.bfloat16), running[1].astype(jnp.bfloat16))
```

```python
import functools
import math

import jax
import jax.numpy as jnp
from jax import lax
from jax.experimental import pallas as pl
from jax.experimental.pallas import tpu as pltpu
from jax.sharding import PartitionSpec as P

MESH = pl.DeviceIdType.MESH
HEADS = 8
HEAD = 64
BLOCK = 256
FEATURES = 512
LEVELS = 4
PAIRS = HEADS // 2
NEAR_UNITS = 3
KEYS = 3 * BLOCK + 3 * LEVELS * 128
CONTRIBUTIONS = 256 + 3 * 192
OUTSIDE = 1e30
bf16 = jnp.bfloat16
f32 = jnp.float32

OWN, LEFT, RIGHT = 0, 1, 2


def dot_nt(a, b):
    return lax.dot_general(a, b, (((1,), (1,)), ((), ())), preferred_element_type=f32)


def dot_nn(a, b):
    return lax.dot_general(a, b, (((1,), (0,)), ((), ())), preferred_element_type=f32)


def level_rows(level):
    return BLOCK >> level


def unit_offset(unit):
    return unit * BLOCK if unit < NEAR_UNITS else 3 * BLOCK + (unit - NEAR_UNITS) * 384


def contribution_base(level):
    return 0 if level == 1 else 256 + (level - 2) * 192


def kernel(
    device_count,
    sub_count,
    q_ref, k_ref, v_ref, g_ref,
    att_ref, dq_ref, dk_ref, dv_ref,
    near, lev1, lev2, lev3, lev4, pieces,
    qm, gm, gt, kt, prob, top, unit_top, total, ot, dqt, factor, delta,
    eye, upsample, average,
    near_grad, own_grad, piece_grad, twin_grad, twin_third, near_in, coarse_in,
    near_send, near_recv, plane_send, plane_recv, twin_send, twin_recv,
    gnear_send, gnear_recv, gplane_send, gplane_recv, gtwin_send, gtwin_recv,
):
    n = device_count
    me = lax.axis_index("seq") * sub_count + lax.axis_index("sub")
    core = lax.rem(me, 2)
    twin = me + 1 - 2 * core
    levels = [lev1, lev2, lev3, lev4]

    def wrapped(device):
        return lax.rem(device + n, n)

    def mesh_id(device):
        return (device // sub_count, lax.rem(device, sub_count))

    def group_size(level):
        return 2 ** (level - 1)

    def chips(level):
        return max(group_size(level) // 2, 1)

    def chip_place(level):
        return lax.rem(me // 2, chips(level))

    def group_targets(level):
        size = group_size(level)
        group = me // size
        count = n // size
        odd = lax.rem(group, 2)
        third = lax.rem(group + 3 - 6 * odd + count, count)
        below = lax.rem(group - 2 + count, count)
        above = lax.rem(group + 2, count)
        return [below * size, above * size, third * size]

    def plane_target(level, start, chip):
        if level == 1:
            return start
        return start + 2 * chip + core

    partners = [twin, wrapped(me - 1 + 2 * core)]
    for level in range(1, LEVELS + 1):
        starts = group_targets(level)[: 2 if level == 1 else 3]
        for start in starts:
            for chip in range(chips(level)):
                partners.append(plane_target(level, start, chip))

    barrier = pltpu.get_barrier_semaphore()
    for partner in partners:
        pl.semaphore_signal(barrier, inc=1, device_id=mesh_id(partner), device_id_type=MESH)

    row = lax.broadcasted_iota(jnp.int32, (BLOCK, BLOCK), 0)
    col = lax.broadcasted_iota(jnp.int32, (BLOCK, BLOCK), 1)
    eye[...] = jnp.where(row == col, 1.0, 0.0).astype(bf16)
    average[...] = jnp.where(row[:128] == col[:128] // 2, 0.5, 0.0).astype(bf16)
    near[OWN, 0] = k_ref[...]
    near[OWN, 1] = v_ref[...]
    for kv in range(2):
        lev1[kv] = dot_nn(average[...], near[OWN, kv]).astype(bf16)
    for level in range(2, LEVELS + 1):
        fine, coarse = levels[level - 2], levels[level - 1]
        rows = level_rows(level)
        for kv in range(2):
            coarse[kv] = dot_nn(average[:rows, : 2 * rows], fine[kv]).astype(bf16)

    pl.semaphore_wait(barrier, len(partners))

    started = []

    def remote(src, dst, send, recv, device):
        copy = pltpu.make_async_remote_copy(
            src_ref=src, dst_ref=dst, send_sem=send, recv_sem=recv,
            device_id=mesh_id(device), device_id_type=MESH,
        )
        copy.start()
        started.append(copy)

    def arrived(ref, sem):
        pltpu.make_async_copy(ref, ref, sem).wait()

    place = 0
    for level in range(LEVELS, 1, -1):
        rows = level_rows(level)
        targets = group_targets(level)
        for slot, start in ((1, targets[0]), (0, targets[1]), (2, targets[2])):
            for chip in range(chips(level)):
                offset = pl.multiple_of(core * 64 + chip_place(level) * rows, 16)
                remote(
                    levels[level - 1],
                    pieces.at[level - 1, slot, :, pl.ds(offset, rows)],
                    plane_send.at[place],
                    plane_recv.at[3 * (level - 1) + slot],
                    plane_target(level, start, chip),
                )
                place += 1
    targets = group_targets(1)
    for slot, start in ((1, targets[0]), (0, targets[1])):
        remote(lev1, pieces.at[0, slot], plane_send.at[place], plane_recv.at[slot], start)
        place += 1
    remote(near.at[OWN], near.at[LEFT], near_send.at[0], near_recv.at[LEFT], wrapped(me + 1))
    remote(near.at[OWN], near.at[RIGHT], near_send.at[1], near_recv.at[RIGHT], wrapped(me - 1))

    lane = lax.broadcasted_iota(jnp.int32, (BLOCK, 128), 1)

    def prepare(pair, carry):
        lanes = pl.ds(pl.multiple_of(pair * 128, 128), 128)
        queries = q_ref[:, lanes].astype(f32) * (1.0 / math.sqrt(HEAD))
        grads = g_ref[:, lanes]
        grads_wide = grads.astype(f32)
        for half in range(2):
            mine = (lane >= 64) if half else (lane < 64)
            qm[2 * pair + half] = jnp.where(mine, queries, 0.0).astype(bf16)
            gm[2 * pair + half] = jnp.where(mine, grads_wide, 0.0).astype(bf16)
        gt[pair] = dot_nt(eye[:128, :128], grads)
        return carry

    lax.fori_loop(0, PAIRS, prepare, 0)

    def forward(load, size, valid, offset, unit, first=False):
        parts = len(valid)
        step = size // parts

        def body(pair, carry):
            lanes = pl.ds(pl.multiple_of(pair * 128, 128), 128)
            keys, values = load(0, lanes), load(1, lanes)
            kt[lanes, offset : offset + size] = dot_nt(eye[:128, :128], keys).astype(bf16)
            values_t = dot_nt(eye[:128, :128], values).astype(bf16)
            for half in range(2):
                head = 2 * pair + half
                scores = dot_nt(keys, qm[head])
                blocks = [scores[i * step : (i + 1) * step] for i in range(parts)]
                high = None
                for block, flag in zip(blocks, valid):
                    peak = jnp.max(block, axis=0, keepdims=True)
                    if flag is not None:
                        peak = jnp.where(flag, peak, -OUTSIDE)
                    high = peak if high is None else jnp.maximum(high, peak)
                if not first:
                    before = top[head]
                    high = jnp.maximum(high, before)
                weights, sums = [], None
                for block, flag in zip(blocks, valid):
                    shift = high if flag is None else jnp.where(flag, high, OUTSIDE)
                    weight = jnp.exp(block - shift)
                    added = jnp.sum(weight, axis=0, keepdims=True)
                    sums = added if sums is None else sums + added
                    weights.append(weight.astype(bf16))
                weight = weights[0] if parts == 1 else jnp.concatenate(weights, axis=0)
                prob[head, offset : offset + size] = weight
                part = dot_nn(values_t[half * 64 : half * 64 + 64], weight)
                if first:
                    total[head] = sums
                    ot[head] = part
                else:
                    fade = jnp.exp(before - high)
                    total[head] = total[head] * fade + sums
                    ot[head] = ot[head] * fade + part
                top[head] = high
                unit_top[unit, head] = high
            return carry

        lax.fori_loop(0, PAIRS, body, 0)

    def near_load(slot):
        return lambda kv, lanes: near[slot, kv, :, lanes]

    def piece_load(level):
        return lambda kv, lanes: jnp.concatenate(
            [pieces[level - 1, slot, kv, :, lanes] for slot in range(3)], axis=0
        )

    far_slot = LEFT + core
    twin_slot = RIGHT - core
    far_valid = jnp.logical_or(
        jnp.logical_and(core == 0, me >= 1), jnp.logical_and(core == 1, me < n - 1)
    )
    level_valid = {}
    for level in range(1, LEVELS + 1):
        size = group_size(level)
        group, count = me // size, n // size
        odd = lax.rem(group, 2)
        third = group + 3 - 6 * odd
        level_valid[level] = [
            group >= 2,
            group + 2 < count,
            jnp.logical_and(third >= 0, third < count),
        ]

    half_rows = pl.ds(pl.multiple_of(core * 64, 64), 64)
    other_rows = pl.ds(pl.multiple_of(64 - core * 64, 64), 64)

    def plane_arrived(level):
        for slot in range(3):
            arrived(
                pieces.at[level - 1, slot, :, half_rows], plane_recv.at[3 * (level - 1) + slot]
            )

    def to_twin(level):
        for slot in range(3):
            ref = pieces.at[level - 1, slot, :, half_rows]
            at = 3 * (level - 1) + slot
            remote(ref, ref, twin_send.at[at], twin_recv.at[at], twin)

    def twin_arrived(level):
        for slot in range(3):
            arrived(
                pieces.at[level - 1, slot, :, other_rows], twin_recv.at[3 * (level - 1) + slot]
            )

    def forward_level(level):
        unit = NEAR_UNITS + level - 1
        forward(piece_load(level), 384, level_valid[level], unit_offset(unit), unit)

    forward(near_load(OWN), BLOCK, [None], unit_offset(0), 0, first=True)
    arrived(near.at[twin_slot], near_recv.at[twin_slot])
    forward(near_load(twin_slot), BLOCK, [None], unit_offset(1), 1)
    plane_arrived(4)
    to_twin(4)
    plane_arrived(3)
    to_twin(3)
    twin_arrived(4)
    forward_level(4)
    plane_arrived(2)
    to_twin(2)
    twin_arrived(3)
    forward_level(3)
    arrived(pieces.at[0, 0], plane_recv.at[0])
    arrived(pieces.at[0, 1], plane_recv.at[1])
    remote(pieces.at[0, core], pieces.at[0, 2], twin_send.at[0], twin_recv.at[0], twin)
    twin_arrived(2)
    forward_level(2)
    arrived(pieces.at[0, 2], twin_recv.at[0])
    forward_level(1)
    arrived(near.at[far_slot], near_recv.at[far_slot])
    forward(near_load(far_slot), BLOCK, [far_valid], unit_offset(2), 2)

    def finish(pair, carry):
        lanes = pl.ds(pl.multiple_of(pair * 128, 128), 128)
        outs = []
        for half in range(2):
            head = 2 * pair + half
            scale = 1.0 / total[head]
            out = ot[head] * scale
            outs.append(out.astype(bf16))
            delta[head] = jnp.sum(
                gt[pair, half * 64 : half * 64 + 64] * out, axis=0, keepdims=True
            )
            high = top[head]
            for unit in range(NEAR_UNITS + LEVELS):
                factor[unit, head] = jnp.exp(unit_top[unit, head] - high) * scale
            dqt[head] = jnp.zeros((HEAD, BLOCK), f32)
        att_ref[:, lanes] = dot_nt(eye[...], jnp.concatenate(outs, axis=0)).astype(bf16)
        return carry

    lax.fori_loop(0, PAIRS, finish, 0)

    def backward(load, size, offset, unit, store):
        def body(pair, carry):
            lanes = pl.ds(pl.multiple_of(pair * 128, 128), 128)
            values = load(1, lanes)
            key_part, value_part = None, None
            for half in range(2):
                head = 2 * pair + half
                wide = prob[head, offset : offset + size].astype(f32) * factor[unit, head]
                dscore = (wide * (dot_nt(values, gm[head]) - delta[head])).astype(bf16)
                key_new = dot_nn(dscore, qm[head])
                value_new = dot_nn(wide.astype(bf16), gm[head])
                key_part = key_new if key_part is None else key_part + key_new
                value_part = value_new if value_part is None else value_part + value_new
                rows = pl.ds(pl.multiple_of(pair * 128 + half * 64, 64), 64)
                dqt[head] += dot_nn(kt[rows, offset : offset + size], dscore)
            store(lanes, key_part, value_part)
            return carry

        lax.fori_loop(0, PAIRS, body, 0)

    def near_store(slot):
        def store(lanes, key_part, value_part):
            near_grad[slot, 0, :, lanes] = key_part.astype(bf16)
            near_grad[slot, 1, :, lanes] = value_part.astype(bf16)
        return store

    def own_store(lanes, key_part, value_part):
        own_grad[0, :, lanes] = key_part
        own_grad[1, :, lanes] = value_part

    def piece_store(level):
        def store(lanes, key_part, value_part):
            for slot in range(3):
                at = slice(slot * 128, slot * 128 + 128)
                piece_grad[level - 1, slot, 0, :, lanes] = key_part[at].astype(bf16)
                piece_grad[level - 1, slot, 1, :, lanes] = value_part[at].astype(bf16)
        return store

    def backward_level(level):
        unit = NEAR_UNITS + level - 1
        backward(piece_load(level), 384, unit_offset(unit), unit, piece_store(level))

    def grads_to_twin(level):
        for slot in range(3):
            at = 3 * (level - 1) + slot
            remote(
                piece_grad.at[level - 1, slot, :, other_rows],
                twin_grad.at[level - 2, slot],
                gtwin_send.at[at], gtwin_recv.at[at], twin,
            )

    def grads_to_owners(level, place):
        rows = level_rows(level)
        for slot in range(3):
            arrived(twin_grad.at[level - 2, slot], gtwin_recv.at[3 * (level - 1) + slot])
            for kv in range(2):
                piece_grad[level - 1, slot, kv, half_rows] = (
                    piece_grad[level - 1, slot, kv, half_rows].astype(f32)
                    + twin_grad[level - 2, slot, kv].astype(f32)
                ).astype(bf16)
        targets = group_targets(level)
        for slot in range(3):
            for chip in range(chips(level)):
                source = pl.multiple_of(core * 64 + chip * rows, 16)
                base = contribution_base(level) + slot * 64
                target = pl.multiple_of(base + chip_place(level) * rows, 16)
                remote(
                    piece_grad.at[level - 1, slot, :, pl.ds(source, rows)],
                    coarse_in.at[:, pl.ds(target, rows)],
                    gplane_send.at[place], gplane_recv.at[level - 1],
                    plane_target(level, targets[slot], chip),
                )
                place += 1
        return place

    backward(near_load(far_slot), BLOCK, unit_offset(2), 2, near_store(1))
    far_device = wrapped(me - 1 + 2 * core)
    remote(near_grad.at[1], near_in.at[1], gnear_send.at[1], gnear_recv.at[1], far_device)
    backward_level(4)
    grads_to_twin(4)
    backward_level(3)
    grads_to_twin(3)
    place = grads_to_owners(4, 0)
    backward_level(2)
    grads_to_twin(2)
    place = grads_to_owners(3, place)
    backward_level(1)
    remote(piece_grad.at[0, 2], twin_third, gtwin_send.at[0], gtwin_recv.at[0], twin)
    place = grads_to_owners(2, place)
    arrived(twin_third, gtwin_recv.at[0])
    for kv in range(2):
        piece_grad[0, core, kv] = (
            piece_grad[0, core, kv].astype(f32) + twin_third[kv].astype(f32)
        ).astype(bf16)
    targets = group_targets(1)
    for slot in range(2):
        remote(
            piece_grad.at[0, slot], coarse_in.at[:, pl.ds(slot * 128, 128)],
            gplane_send.at[place], gplane_recv.at[0], targets[slot],
        )
        place += 1
    backward(near_load(twin_slot), BLOCK, unit_offset(1), 1, near_store(0))
    remote(near_grad.at[0], near_in.at[0], gnear_send.at[0], gnear_recv.at[0], twin)
    backward(near_load(OWN), BLOCK, unit_offset(0), 0, own_store)

    def write_queries(pair, carry):
        lanes = pl.ds(pl.multiple_of(pair * 128, 128), 128)
        both = jnp.concatenate([dqt[2 * pair], dqt[2 * pair + 1]], axis=0)
        both = (both * (1.0 / math.sqrt(HEAD))).astype(bf16)
        dq_ref[:, lanes] = dot_nt(eye[...], both).astype(bf16)
        return carry

    lax.fori_loop(0, PAIRS, write_queries, 0)

    for level in range(1, LEVELS + 1):
        count = 128 if level == 1 else level_rows(level)
        base = contribution_base(level)
        width = 256 if level == 1 else 192
        r = lax.broadcasted_iota(jnp.int32, (BLOCK, width), 0)
        c = lax.broadcasted_iota(jnp.int32, (BLOCK, width), 1)
        upsample[:, base : base + width] = jnp.where(
            lax.rem(c, count) == r // 2**level, 0.5**level, 0.0
        ).astype(bf16)
    arrived(near_in.at[0], gnear_recv.at[0])
    arrived(near_in.at[1], gnear_recv.at[1])
    for level in range(LEVELS, 0, -1):
        width = 256 if level == 1 else 192
        arrived(
            coarse_in.at[:, pl.ds(contribution_base(level), width)], gplane_recv.at[level - 1]
        )
    for kv, out_ref in ((0, dk_ref), (1, dv_ref)):
        def write(pair, carry):
            lanes = pl.ds(pl.multiple_of(pair * 128, 128), 128)
            out = own_grad[kv, :, lanes] + near_in[0, kv, :, lanes].astype(f32)
            out = out + near_in[1, kv, :, lanes].astype(f32)
            out = out + dot_nn(upsample[...], coarse_in[kv, :, lanes])
            out_ref[:, lanes] = out.astype(bf16)
            return carry

        lax.fori_loop(0, PAIRS, write, 0)

    for copy in started:
        copy.wait_send()


def on_device(device_count, sub_count, queries, keys, values, cotangent):
    vmem = pl.BlockSpec(memory_space=pltpu.VMEM)
    dma = pltpu.SemaphoreType.DMA
    rows = (BLOCK, FEATURES)
    plane_messages = 2 + 3 + 6 + 12
    scratch = [
        pltpu.VMEM((3, 2) + rows, bf16),
        pltpu.VMEM((2, 128, FEATURES), bf16),
        pltpu.VMEM((2, 64, FEATURES), bf16),
        pltpu.VMEM((2, 32, FEATURES), bf16),
        pltpu.VMEM((2, 16, FEATURES), bf16),
        pltpu.VMEM((LEVELS, 3, 2, 128, FEATURES), bf16),
        pltpu.VMEM((HEADS, BLOCK, 128), bf16),
        pltpu.VMEM((HEADS, BLOCK, 128), bf16),
        pltpu.VMEM((PAIRS, 128, BLOCK), f32),
        pltpu.VMEM((FEATURES, KEYS), bf16),
        pltpu.VMEM((HEADS, KEYS, BLOCK), bf16),
        pltpu.VMEM((HEADS, 1, BLOCK), f32),
        pltpu.VMEM((NEAR_UNITS + LEVELS, HEADS, 1, BLOCK), f32),
        pltpu.VMEM((HEADS, 1, BLOCK), f32),
        pltpu.VMEM((HEADS, HEAD, BLOCK), f32),
        pltpu.VMEM((HEADS, HEAD, BLOCK), f32),
        pltpu.VMEM((NEAR_UNITS + LEVELS, HEADS, 1, BLOCK), f32),
        pltpu.VMEM((HEADS, 1, BLOCK), f32),
        pltpu.VMEM((BLOCK, BLOCK), bf16),
        pltpu.VMEM((BLOCK, CONTRIBUTIONS), bf16),
        pltpu.VMEM((128, BLOCK), bf16),
        pltpu.VMEM((2, 2) + rows, bf16),
        pltpu.VMEM((2,) + rows, f32),
        pltpu.VMEM((LEVELS, 3, 2, 128, FEATURES), bf16),
        pltpu.VMEM((LEVELS - 1, 3, 2, 64, FEATURES), bf16),
        pltpu.VMEM((2, 128, FEATURES), bf16),
        pltpu.VMEM((2, 2) + rows, bf16),
        pltpu.VMEM((2, CONTRIBUTIONS, FEATURES), bf16),
        dma((2,)), dma((3,)),
        dma((plane_messages,)), dma((3 * LEVELS,)),
        dma((3 * LEVELS,)), dma((3 * LEVELS,)),
        dma((2,)), dma((2,)),
        dma((plane_messages,)), dma((LEVELS,)),
        dma((3 * LEVELS,)), dma((3 * LEVELS,)),
    ]
    return pl.pallas_call(
        functools.partial(kernel, device_count, sub_count),
        out_shape=[jax.ShapeDtypeStruct(rows, bf16)] * 4,
        in_specs=[vmem] * 4,
        out_specs=[vmem] * 4,
        scratch_shapes=scratch,
        compiler_params=pltpu.CompilerParams(
            collective_id=0, has_side_effects=True, vmem_limit_bytes=56 * 2**20
        ),
        name="hierarchical_attention",
    )(queries, keys, values, cotangent)


def solution(mesh):
    spec = P(("seq", "sub"), None)
    device_count = mesh.shape["seq"] * mesh.shape["sub"]
    return jax.shard_map(
        functools.partial(on_device, device_count, mesh.shape["sub"]),
        mesh=mesh,
        in_specs=(spec,) * 4,
        out_specs=(spec,) * 4,
        check_vma=False,
    )
```

```python
import functools
import math

import jax
import jax.numpy as jnp
from jax import lax
from jax.experimental import pallas as pl
from jax.experimental.pallas import tpu as pltpu
from jax.sharding import PartitionSpec as P

MESH = pl.DeviceIdType.MESH
HEADS = 8
HEAD = 64
BLOCK = 256
FEATURES = 512
LEVELS = 4
PAIRS = HEADS // 2
NEAR_UNITS = 3
KEYS = 3 * BLOCK + 3 * LEVELS * 128
CONTRIBUTIONS = 256 + 3 * 192
OUTSIDE = 1e30
bf16 = jnp.bfloat16
f32 = jnp.float32

OWN, LEFT, RIGHT = 0, 1, 2


def dot_nt(a, b):
    return lax.dot_general(a, b, (((1,), (1,)), ((), ())), preferred_element_type=f32)


def dot_tn(a, b):
    return lax.dot_general(a, b, (((0,), (0,)), ((), ())), preferred_element_type=f32)


def dot_nn(a, b):
    return lax.dot_general(a, b, (((1,), (0,)), ((), ())), preferred_element_type=f32)


def level_rows(level):
    return BLOCK >> level


def unit_offset(unit):
    return unit * BLOCK if unit < NEAR_UNITS else 3 * BLOCK + (unit - NEAR_UNITS) * 384


def contribution_base(level):
    return 0 if level == 1 else 256 + (level - 2) * 192


def kernel(
    device_count,
    sub_count,
    q_ref, k_ref, v_ref, g_ref,
    att_ref, dq_ref, dk_ref, dv_ref,
    near, lev1, lev2, lev3, lev4, pieces,
    qm, gm, prob, top, total, out_part, dq_part, factor, delta,
    upsample, average,
    near_grad, own_grad, piece_grad, twin_grad, twin_third, near_in, coarse_in,
    near_send, near_recv, plane_send, plane_recv, twin_send, twin_recv,
    gnear_send, gnear_recv, gplane_send, gplane_recv, gtwin_send, gtwin_recv,
):
    n = device_count
    me = lax.axis_index("seq") * sub_count + lax.axis_index("sub")
    core = lax.rem(me, 2)
    twin = me + 1 - 2 * core
    levels = [lev1, lev2, lev3, lev4]

    def wrapped(device):
        return lax.rem(device + n, n)

    def mesh_id(device):
        return (device // sub_count, lax.rem(device, sub_count))

    def group_size(level):
        return 2 ** (level - 1)

    def chips(level):
        return max(group_size(level) // 2, 1)

    def chip_place(level):
        return lax.rem(me // 2, chips(level))

    def group_targets(level):
        size = group_size(level)
        group = me // size
        count = n // size
        odd = lax.rem(group, 2)
        third = lax.rem(group + 3 - 6 * odd + count, count)
        below = lax.rem(group - 2 + count, count)
        above = lax.rem(group + 2, count)
        return [below * size, above * size, third * size]

    def plane_target(level, start, chip):
        if level == 1:
            return start
        return start + 2 * chip + core

    partners = [twin, wrapped(me - 1 + 2 * core)]
    for level in range(1, LEVELS + 1):
        starts = group_targets(level)[: 2 if level == 1 else 3]
        for start in starts:
            for chip in range(chips(level)):
                partners.append(plane_target(level, start, chip))

    barrier = pltpu.get_barrier_semaphore()
    for partner in partners:
        pl.semaphore_signal(barrier, inc=1, device_id=mesh_id(partner), device_id_type=MESH)

    row = lax.broadcasted_iota(jnp.int32, (BLOCK, BLOCK), 0)
    col = lax.broadcasted_iota(jnp.int32, (BLOCK, BLOCK), 1)
    average[...] = jnp.where(row[:128] == col[:128] // 2, 0.5, 0.0).astype(bf16)
    near[OWN, 0] = k_ref[...]
    near[OWN, 1] = v_ref[...]
    for kv in range(2):
        lev1[kv] = dot_nn(average[...], near[OWN, kv]).astype(bf16)
    for level in range(2, LEVELS + 1):
        fine, coarse = levels[level - 2], levels[level - 1]
        rows = level_rows(level)
        for kv in range(2):
            coarse[kv] = dot_nn(average[:rows, : 2 * rows], fine[kv]).astype(bf16)

    pl.semaphore_wait(barrier, len(partners))

    started = []

    def remote(src, dst, send, recv, device):
        copy = pltpu.make_async_remote_copy(
            src_ref=src, dst_ref=dst, send_sem=send, recv_sem=recv,
            device_id=mesh_id(device), device_id_type=MESH,
        )
        copy.start()
        started.append(copy)

    def arrived(ref, sem):
        pltpu.make_async_copy(ref, ref, sem).wait()

    place = 0
    for level in range(LEVELS, 1, -1):
        rows = level_rows(level)
        targets = group_targets(level)
        for slot, start in ((1, targets[0]), (0, targets[1]), (2, targets[2])):
            for chip in range(chips(level)):
                offset = pl.multiple_of(core * 64 + chip_place(level) * rows, 16)
                remote(
                    levels[level - 1],
                    pieces.at[level - 1, slot, :, pl.ds(offset, rows)],
                    plane_send.at[place],
                    plane_recv.at[3 * (level - 1) + slot],
                    plane_target(level, start, chip),
                )
                place += 1
    targets = group_targets(1)
    for slot, start in ((1, targets[0]), (0, targets[1])):
        remote(lev1, pieces.at[0, slot], plane_send.at[place], plane_recv.at[slot], start)
        place += 1
    remote(near.at[OWN], near.at[LEFT], near_send.at[0], near_recv.at[LEFT], wrapped(me + 1))
    remote(near.at[OWN], near.at[RIGHT], near_send.at[1], near_recv.at[RIGHT], wrapped(me - 1))

    lane = lax.broadcasted_iota(jnp.int32, (BLOCK, 128), 1)

    def prepare(pair, carry):
        lanes = pl.ds(pl.multiple_of(pair * 128, 128), 128)
        queries = q_ref[:, lanes].astype(f32) * (1.0 / math.sqrt(HEAD))
        grads = g_ref[:, lanes]
        grads_wide = grads.astype(f32)
        for half in range(2):
            mine = (lane >= 64) if half else (lane < 64)
            qm[2 * pair + half] = jnp.where(mine, queries, 0.0).astype(bf16)
            gm[2 * pair + half] = jnp.where(mine, grads_wide, 0.0).astype(bf16)
        return carry

    lax.fori_loop(0, PAIRS, prepare, 0)

    first_head = lane < 64

    def forward(load, size, valid, offset, unit):
        parts = len(valid)
        step = size // parts

        def body(pair, carry):
            lanes = pl.ds(pl.multiple_of(pair * 128, 128), 128)
            keys, values = load(0, lanes), load(1, lanes)
            outs = []
            for half in range(2):
                head = 2 * pair + half
                scores = dot_nt(keys, qm[head])
                blocks = [scores[i * step : (i + 1) * step] for i in range(parts)]
                high = None
                for block, flag in zip(blocks, valid):
                    peak = jnp.max(block, axis=0, keepdims=True)
                    if flag is not None:
                        peak = jnp.where(flag, peak, -OUTSIDE)
                    high = peak if high is None else jnp.maximum(high, peak)
                weights, sums = [], None
                for block, flag in zip(blocks, valid):
                    shift = high if flag is None else jnp.where(flag, high, OUTSIDE)
                    weight = jnp.exp(block - shift)
                    added = jnp.sum(weight, axis=0, keepdims=True)
                    sums = added if sums is None else sums + added
                    weights.append(weight.astype(bf16))
                weight = weights[0] if parts == 1 else jnp.concatenate(weights, axis=0)
                prob[head, offset : offset + size] = weight
                outs.append(dot_tn(weight, values))
                top[unit, head] = high
                total[unit, head] = sums
            out_part[unit, pair] = jnp.where(first_head, outs[0], outs[1])
            return carry

        lax.fori_loop(0, PAIRS, body, 0, unroll=True)

    def near_load(slot):
        return lambda kv, lanes: near[slot, kv, :, lanes]

    def piece_load(level):
        return lambda kv, lanes: jnp.concatenate(
            [pieces[level - 1, slot, kv, :, lanes] for slot in range(3)], axis=0
        )

    far_slot = LEFT + core
    twin_slot = RIGHT - core
    far_valid = jnp.logical_or(
        jnp.logical_and(core == 0, me >= 1), jnp.logical_and(core == 1, me < n - 1)
    )
    level_valid = {}
    for level in range(1, LEVELS + 1):
        size = group_size(level)
        group, count = me // size, n // size
        odd = lax.rem(group, 2)
        third = group + 3 - 6 * odd
        level_valid[level] = [
            group >= 2,
            group + 2 < count,
            jnp.logical_and(third >= 0, third < count),
        ]

    half_rows = pl.ds(pl.multiple_of(core * 64, 64), 64)
    other_rows = pl.ds(pl.multiple_of(64 - core * 64, 64), 64)

    def plane_arrived(level):
        for slot in range(3):
            arrived(
                pieces.at[level - 1, slot, :, half_rows], plane_recv.at[3 * (level - 1) + slot]
            )

    def to_twin(level):
        for slot in range(3):
            ref = pieces.at[level - 1, slot, :, half_rows]
            at = 3 * (level - 1) + slot
            remote(ref, ref, twin_send.at[at], twin_recv.at[at], twin)

    def twin_arrived(level):
        for slot in range(3):
            arrived(
                pieces.at[level - 1, slot, :, other_rows], twin_recv.at[3 * (level - 1) + slot]
            )

    def forward_level(level):
        unit = NEAR_UNITS + level - 1
        forward(piece_load(level), 384, level_valid[level], unit_offset(unit), unit)

    forward(near_load(OWN), BLOCK, [None], unit_offset(0), 0)
    arrived(near.at[twin_slot], near_recv.at[twin_slot])
    forward(near_load(twin_slot), BLOCK, [None], unit_offset(1), 1)
    plane_arrived(4)
    to_twin(4)
    plane_arrived(3)
    to_twin(3)
    twin_arrived(4)
    forward_level(4)
    plane_arrived(2)
    to_twin(2)
    twin_arrived(3)
    forward_level(3)
    arrived(pieces.at[0, 0], plane_recv.at[0])
    arrived(pieces.at[0, 1], plane_recv.at[1])
    remote(pieces.at[0, core], pieces.at[0, 2], twin_send.at[0], twin_recv.at[0], twin)
    twin_arrived(2)
    forward_level(2)
    arrived(pieces.at[0, 2], twin_recv.at[0])
    forward_level(1)
    arrived(near.at[far_slot], near_recv.at[far_slot])
    forward(near_load(far_slot), BLOCK, [far_valid], unit_offset(2), 2)

    units = range(NEAR_UNITS + LEVELS)
    head_row = lax.broadcasted_iota(jnp.int32, (8, 128), 0)
    head_lane = lax.broadcasted_iota(jnp.int32, (8, 128), 1) // 64
    head_sum = jnp.where(head_row == head_lane, 1.0, 0.0).astype(bf16)

    def finish(pair, carry):
        lanes = pl.ds(pl.multiple_of(pair * 128, 128), 128)
        rows = []
        for half in range(2):
            head = 2 * pair + half
            high = functools.reduce(jnp.maximum, [top[unit, head] for unit in units])
            fades = [jnp.exp(top[unit, head] - high) for unit in units]
            scale = 1.0 / sum(fade * total[unit, head] for unit, fade in zip(units, fades))
            for unit, fade in zip(units, fades):
                factor[unit, head] = fade * scale
                rows.append(fade * scale)
        rows += [jnp.zeros_like(rows[0])] * (16 - len(rows))
        columns = jnp.transpose(jnp.concatenate(rows, axis=0))
        out = None
        for unit in units:
            second = len(units) + unit
            both = jnp.where(
                first_head, columns[:, unit : unit + 1], columns[:, second : second + 1]
            )
            added = out_part[unit, pair] * both
            out = added if out is None else out + added
        att_ref[:, lanes] = out.astype(bf16)
        product = out * g_ref[:, lanes].astype(f32)
        coarse = product.astype(bf16)
        rest = (product - coarse.astype(f32)).astype(bf16)
        deltas = dot_nt(head_sum, coarse) + dot_nt(head_sum, rest)
        for half in range(2):
            delta[2 * pair + half] = deltas[half : half + 1]
            dq_part[2 * pair + half] = jnp.zeros((BLOCK, 128), f32)
        return carry

    lax.fori_loop(0, PAIRS, finish, 0, unroll=True)

    def backward(load, size, offset, unit, store):
        def body(pair, carry):
            lanes = pl.ds(pl.multiple_of(pair * 128, 128), 128)
            keys, values = load(0, lanes), load(1, lanes)
            key_part, value_part = None, None
            for half in range(2):
                head = 2 * pair + half
                wide = prob[head, offset : offset + size].astype(f32) * factor[unit, head]
                dscore = (wide * (dot_nt(values, gm[head]) - delta[head])).astype(bf16)
                key_new = dot_nn(dscore, qm[head])
                value_new = dot_nn(wide.astype(bf16), gm[head])
                key_part = key_new if key_part is None else key_part + key_new
                value_part = value_new if value_part is None else value_part + value_new
                dq_part[head] += dot_tn(dscore, keys)
            store(lanes, key_part, value_part)
            return carry

        lax.fori_loop(0, PAIRS, body, 0, unroll=True)

    def near_store(slot):
        def store(lanes, key_part, value_part):
            near_grad[slot, 0, :, lanes] = key_part.astype(bf16)
            near_grad[slot, 1, :, lanes] = value_part.astype(bf16)
        return store

    def own_store(lanes, key_part, value_part):
        own_grad[0, :, lanes] = key_part
        own_grad[1, :, lanes] = value_part

    def piece_store(level):
        def store(lanes, key_part, value_part):
            for slot in range(3):
                at = slice(slot * 128, slot * 128 + 128)
                piece_grad[level - 1, slot, 0, :, lanes] = key_part[at].astype(bf16)
                piece_grad[level - 1, slot, 1, :, lanes] = value_part[at].astype(bf16)
        return store

    def backward_level(level):
        unit = NEAR_UNITS + level - 1
        backward(piece_load(level), 384, unit_offset(unit), unit, piece_store(level))

    def grads_to_twin(level):
        for slot in range(3):
            at = 3 * (level - 1) + slot
            remote(
                piece_grad.at[level - 1, slot, :, other_rows],
                twin_grad.at[level - 2, slot],
                gtwin_send.at[at], gtwin_recv.at[at], twin,
            )

    def grads_to_owners(level, place):
        rows = level_rows(level)
        for slot in range(3):
            arrived(twin_grad.at[level - 2, slot], gtwin_recv.at[3 * (level - 1) + slot])
            for kv in range(2):
                piece_grad[level - 1, slot, kv, half_rows] = (
                    piece_grad[level - 1, slot, kv, half_rows].astype(f32)
                    + twin_grad[level - 2, slot, kv].astype(f32)
                ).astype(bf16)
        targets = group_targets(level)
        for slot in range(3):
            for chip in range(chips(level)):
                source = pl.multiple_of(core * 64 + chip * rows, 16)
                base = contribution_base(level) + slot * 64
                target = pl.multiple_of(base + chip_place(level) * rows, 16)
                remote(
                    piece_grad.at[level - 1, slot, :, pl.ds(source, rows)],
                    coarse_in.at[:, pl.ds(target, rows)],
                    gplane_send.at[place], gplane_recv.at[level - 1],
                    plane_target(level, targets[slot], chip),
                )
                place += 1
        return place

    backward(near_load(far_slot), BLOCK, unit_offset(2), 2, near_store(1))
    far_device = wrapped(me - 1 + 2 * core)
    remote(near_grad.at[1], near_in.at[1], gnear_send.at[1], gnear_recv.at[1], far_device)
    backward_level(4)
    grads_to_twin(4)
    backward_level(3)
    grads_to_twin(3)
    place = grads_to_owners(4, 0)
    backward_level(2)
    grads_to_twin(2)
    place = grads_to_owners(3, place)
    backward_level(1)
    remote(piece_grad.at[0, 2], twin_third, gtwin_send.at[0], gtwin_recv.at[0], twin)
    place = grads_to_owners(2, place)
    arrived(twin_third, gtwin_recv.at[0])
    for kv in range(2):
        piece_grad[0, core, kv] = (
            piece_grad[0, core, kv].astype(f32) + twin_third[kv].astype(f32)
        ).astype(bf16)
    targets = group_targets(1)
    for slot in range(2):
        remote(
            piece_grad.at[0, slot], coarse_in.at[:, pl.ds(slot * 128, 128)],
            gplane_send.at[place], gplane_recv.at[0], targets[slot],
        )
        place += 1
    backward(near_load(twin_slot), BLOCK, unit_offset(1), 1, near_store(0))
    remote(near_grad.at[0], near_in.at[0], gnear_send.at[0], gnear_recv.at[0], twin)
    backward(near_load(OWN), BLOCK, unit_offset(0), 0, own_store)

    def write_queries(pair, carry):
        lanes = pl.ds(pl.multiple_of(pair * 128, 128), 128)
        both = jnp.where(first_head, dq_part[2 * pair], dq_part[2 * pair + 1])
        dq_ref[:, lanes] = (both * (1.0 / math.sqrt(HEAD))).astype(bf16)
        return carry

    lax.fori_loop(0, PAIRS, write_queries, 0)

    for level in range(1, LEVELS + 1):
        count = 128 if level == 1 else level_rows(level)
        base = contribution_base(level)
        width = 256 if level == 1 else 192
        r = lax.broadcasted_iota(jnp.int32, (BLOCK, width), 0)
        c = lax.broadcasted_iota(jnp.int32, (BLOCK, width), 1)
        upsample[:, base : base + width] = jnp.where(
            lax.rem(c, count) == r // 2**level, 0.5**level, 0.0
        ).astype(bf16)
    arrived(near_in.at[0], gnear_recv.at[0])
    arrived(near_in.at[1], gnear_recv.at[1])
    for level in range(LEVELS, 0, -1):
        width = 256 if level == 1 else 192
        arrived(
            coarse_in.at[:, pl.ds(contribution_base(level), width)], gplane_recv.at[level - 1]
        )
    for kv, out_ref in ((0, dk_ref), (1, dv_ref)):
        def write(pair, carry):
            lanes = pl.ds(pl.multiple_of(pair * 128, 128), 128)
            out = own_grad[kv, :, lanes] + near_in[0, kv, :, lanes].astype(f32)
            out = out + near_in[1, kv, :, lanes].astype(f32)
            out = out + dot_nn(upsample[...], coarse_in[kv, :, lanes])
            out_ref[:, lanes] = out.astype(bf16)
            return carry

        lax.fori_loop(0, PAIRS, write, 0)

    for copy in started:
        copy.wait_send()


def hand_over(*refs):
    sources, targets, (held, in_sem, out_sem) = refs[:4], refs[4:8], refs[8:]
    inward = [
        pltpu.make_async_copy(source, held.at[i], in_sem.at[i]) for i, source in enumerate(sources)
    ]
    outward = [
        pltpu.make_async_copy(held.at[i], target, out_sem.at[i]) for i, target in enumerate(targets)
    ]
    for copy in inward:
        copy.start()
    for first, second in zip(inward, outward):
        first.wait()
        second.start()
    for copy in outward:
        copy.wait()


def on_device(device_count, sub_count, queries, keys, values, cotangent):
    vmem = pl.BlockSpec(memory_space=pltpu.VMEM)
    dma = pltpu.SemaphoreType.DMA
    rows = (BLOCK, FEATURES)
    plane_messages = 2 + 3 + 6 + 12
    scratch = [
        pltpu.VMEM((3, 2) + rows, bf16),
        pltpu.VMEM((2, 128, FEATURES), bf16),
        pltpu.VMEM((2, 64, FEATURES), bf16),
        pltpu.VMEM((2, 32, FEATURES), bf16),
        pltpu.VMEM((2, 16, FEATURES), bf16),
        pltpu.VMEM((LEVELS, 3, 2, 128, FEATURES), bf16),
        pltpu.VMEM((HEADS, BLOCK, 128), bf16),
        pltpu.VMEM((HEADS, BLOCK, 128), bf16),
        pltpu.VMEM((HEADS, KEYS, BLOCK), bf16),
        pltpu.VMEM((NEAR_UNITS + LEVELS, HEADS, 1, BLOCK), f32),
        pltpu.VMEM((NEAR_UNITS + LEVELS, HEADS, 1, BLOCK), f32),
        pltpu.VMEM((NEAR_UNITS + LEVELS, PAIRS, BLOCK, 128), f32),
        pltpu.VMEM((HEADS, BLOCK, 128), f32),
        pltpu.VMEM((NEAR_UNITS + LEVELS, HEADS, 1, BLOCK), f32),
        pltpu.VMEM((HEADS, 1, BLOCK), f32),
        pltpu.VMEM((BLOCK, CONTRIBUTIONS), bf16),
        pltpu.VMEM((128, BLOCK), bf16),
        pltpu.VMEM((2, 2) + rows, bf16),
        pltpu.VMEM((2,) + rows, f32),
        pltpu.VMEM((LEVELS, 3, 2, 128, FEATURES), bf16),
        pltpu.VMEM((LEVELS - 1, 3, 2, 64, FEATURES), bf16),
        pltpu.VMEM((2, 128, FEATURES), bf16),
        pltpu.VMEM((2, 2) + rows, bf16),
        pltpu.VMEM((2, CONTRIBUTIONS, FEATURES), bf16),
        dma((2,)), dma((3,)),
        dma((plane_messages,)), dma((3 * LEVELS,)),
        dma((3 * LEVELS,)), dma((3 * LEVELS,)),
        dma((2,)), dma((2,)),
        dma((plane_messages,)), dma((LEVELS,)),
        dma((3 * LEVELS,)), dma((3 * LEVELS,)),
    ]
    results = pl.pallas_call(
        functools.partial(kernel, device_count, sub_count),
        out_shape=[jax.ShapeDtypeStruct(rows, bf16)] * 4,
        in_specs=[vmem] * 4,
        out_specs=[vmem] * 4,
        scratch_shapes=scratch,
        compiler_params=pltpu.CompilerParams(
            collective_id=0, has_side_effects=True, vmem_limit_bytes=56 * 2**20
        ),
        name="hierarchical_attention",
    )(queries, keys, values, cotangent)
    anywhere = pl.BlockSpec(memory_space=pl.ANY)
    return pl.pallas_call(
        hand_over,
        out_shape=[jax.ShapeDtypeStruct(rows, bf16)] * 4,
        in_specs=[anywhere] * 4,
        out_specs=[anywhere] * 4,
        scratch_shapes=[pltpu.VMEM((4,) + rows, bf16), dma((4,)), dma((4,))],
        name="hand_over",
    )(*results)


def solution(mesh):
    spec = P(("seq", "sub"), None)
    device_count = mesh.shape["seq"] * mesh.shape["sub"]
    return jax.shard_map(
        functools.partial(on_device, device_count, mesh.shape["sub"]),
        mesh=mesh,
        in_specs=(spec,) * 4,
        out_specs=(spec,) * 4,
        check_vma=False,
    )
```

```python
import functools
import math

import jax
import jax.numpy as jnp
from jax import lax
from jax.experimental import pallas as pl
from jax.experimental.pallas import tpu as pltpu
from jax.sharding import PartitionSpec as P

MESH = pl.DeviceIdType.MESH
HEADS = 8
HEAD = 64
BLOCK = 256
FEATURES = 512
LEVELS = 4
PAIRS = HEADS // 2
NEAR_UNITS = 3
KEYS = 3 * BLOCK + 3 * LEVELS * 128
CONTRIBUTIONS = 128 + 2 * 192 + 64
OUTSIDE = 1e30
bf16 = jnp.bfloat16
f32 = jnp.float32

OWN, LEFT, RIGHT = 0, 1, 2


def dot_nt(a, b):
    return lax.dot_general(a, b, (((1,), (1,)), ((), ())), preferred_element_type=f32)


def dot_tn(a, b):
    return lax.dot_general(a, b, (((0,), (0,)), ((), ())), preferred_element_type=f32)


def dot_nn(a, b):
    return lax.dot_general(a, b, (((1,), (0,)), ((), ())), preferred_element_type=f32)


def level_rows(level):
    return BLOCK >> level


def unit_offset(unit):
    return unit * BLOCK if unit < NEAR_UNITS else 3 * BLOCK + (unit - NEAR_UNITS) * 384


def contribution_base(level):
    return (0, 128, 320, 512)[level - 1]


def contribution_width(level):
    return (128, 192, 192, 64)[level - 1]


def kernel(
    device_count,
    sub_count,
    q_ref, k_ref, v_ref, g_ref,
    att_ref, dq_ref, dk_ref, dv_ref,
    near, lev1, lev2, lev3, lev4, pieces,
    qm, gm, prob, top, total, out_part, dq_part, factor, delta,
    upsample, average,
    near_grad, own_grad, piece_grad, twin_grad, twin_first, near_in, coarse_in,
    row_keys, row_grads, row_sum, derived,
    near_send, near_recv, plane_send, plane_recv, twin_send, twin_recv,
    gnear_send, gnear_recv, gplane_send, gplane_recv, gtwin_send, gtwin_recv,
    row_send, row_recv, grow_send, grow_recv,
):
    n = device_count
    me = lax.axis_index("seq") * sub_count + lax.axis_index("sub")
    core = lax.rem(me, 2)
    twin = me + 1 - 2 * core
    levels = [lev1, lev2, lev3, lev4]

    def wrapped(device):
        return lax.rem(device + n, n)

    def mesh_id(device):
        return (device // sub_count, lax.rem(device, sub_count))

    def group_size(level):
        return 2 ** (level - 1)

    def chips(level):
        return max(group_size(level) // 2, 1)

    def chip_place(level):
        return lax.rem(me // 2, chips(level))

    def group_targets(level):
        size = group_size(level)
        group = me // size
        count = n // size
        odd = lax.rem(group, 2)
        third = lax.rem(group + 3 - 6 * odd + count, count)
        below = lax.rem(group - 2 + count, count)
        above = lax.rem(group + 2, count)
        return [below * size, above * size, third * size]

    row_place = lax.rem(me // 2, 4)
    row_start = me - lax.rem(me, 8)

    def plane_chips(level):
        return 1 if level == 4 else chips(level)

    def plane_target(level, start, chip):
        if level == 1:
            return start
        if level == 4:
            return start + lax.rem(me, 8)
        return start + 2 * chip + core

    def row_partner(step):
        place = lax.rem(row_place + step, 4)
        return place, row_start + 2 * place + core

    partners = [twin, wrapped(me - 1 + 2 * core)]
    for level in range(1, LEVELS + 1):
        starts = group_targets(level)[: 2 if level == 1 else 3]
        for start in starts:
            for chip in range(plane_chips(level)):
                partners.append(plane_target(level, start, chip))
    partners += [row_partner(step)[1] for step in (1, 2, 3)]

    barrier = pltpu.get_barrier_semaphore()
    for partner in partners:
        pl.semaphore_signal(barrier, inc=1, device_id=mesh_id(partner), device_id_type=MESH)

    row = lax.broadcasted_iota(jnp.int32, (BLOCK, BLOCK), 0)
    col = lax.broadcasted_iota(jnp.int32, (BLOCK, BLOCK), 1)
    average[...] = jnp.where(row[:128] == col[:128] // 2, 0.5, 0.0).astype(bf16)
    near[OWN, 0] = k_ref[...]
    near[OWN, 1] = v_ref[...]
    for kv in range(2):
        lev1[kv] = dot_nn(average[...], near[OWN, kv]).astype(bf16)
    for level in range(2, LEVELS + 1):
        fine, coarse = levels[level - 2], levels[level - 1]
        rows = level_rows(level)
        for kv in range(2):
            coarse[kv] = dot_nn(average[:rows, : 2 * rows], fine[kv]).astype(bf16)
    own_row = pl.ds(pl.multiple_of(row_place * 16, 16), 16)
    for kv in range(2):
        row_keys[kv, own_row] = lev4[kv]

    pl.semaphore_wait(barrier, len(partners))

    started = []

    def remote(src, dst, send, recv, device):
        copy = pltpu.make_async_remote_copy(
            src_ref=src, dst_ref=dst, send_sem=send, recv_sem=recv,
            device_id=mesh_id(device), device_id_type=MESH,
        )
        copy.start()
        started.append(copy)

    def arrived(ref, sem):
        pltpu.make_async_copy(ref, ref, sem).wait()

    def group_lanes(part):
        return pl.ds(part * 256, 256)

    for step in (1, 3, 2):
        remote(
            lev4, row_keys.at[:, own_row], row_send.at[step - 1], row_recv.at[step - 1],
            row_partner(step)[1],
        )
    far_slot = LEFT + core
    twin_slot = RIGHT - core
    far_device = wrapped(me - 1 + 2 * core)
    half_rows = pl.ds(pl.multiple_of(core * 64, 64), 64)
    other_rows = pl.ds(pl.multiple_of(64 - core * 64, 64), 64)

    def send_keys(part):
        lanes = group_lanes(part)
        block = near.at[OWN, :, :, lanes]
        remote(
            block, near.at[RIGHT - core, :, :, lanes],
            near_send.at[part, 0], near_recv.at[part, 0], far_device,
        )
        remote(
            block, near.at[LEFT + core, :, :, lanes],
            near_send.at[part, 1], near_recv.at[part, 1], twin,
        )
        place = 0
        for level in (3, 2):
            rows = level_rows(level)
            targets = group_targets(level)
            for slot, start in ((1, targets[0]), (0, targets[1]), (2, targets[2])):
                for chip in range(chips(level)):
                    offset = pl.multiple_of(core * 64 + chip_place(level) * rows, 16)
                    remote(
                        levels[level - 1].at[:, :, lanes],
                        pieces.at[level - 1, slot, :, pl.ds(offset, rows), lanes],
                        plane_send.at[part, place],
                        plane_recv.at[part, 3 * (level - 1) + slot],
                        plane_target(level, start, chip),
                    )
                    place += 1
        remote(
            lev1.at[:, :, lanes], pieces.at[0, core, :, :, lanes],
            plane_send.at[part, place], plane_recv.at[part, 0], wrapped(me + 2 - 4 * core),
        )

    def send_row(part):
        lanes = group_lanes(part)
        targets = group_targets(4)
        for slot, start in ((1, targets[0]), (0, targets[1]), (2, targets[2])):
            remote(
                row_keys.at[:, :, lanes], pieces.at[3, slot, :, half_rows, lanes],
                plane_send.at[part, 10 + slot], plane_recv.at[part, 9 + slot],
                plane_target(4, start, 0),
            )

    send_keys(0)
    for step in (1, 3, 2):
        from_place = lax.rem(row_place + 4 - step, 4)
        arrived(
            row_keys.at[:, pl.ds(pl.multiple_of(from_place * 16, 16), 16)], row_recv.at[step - 1]
        )
    send_row(0)
    send_keys(1)
    send_row(1)

    lane = lax.broadcasted_iota(jnp.int32, (BLOCK, 128), 1)
    first_head = lane < 64

    def pairs_of(part):
        return range(2 * part, 2 * part + 2)

    def pair_lanes(pair):
        return slice(pair * 128, pair * 128 + 128)

    for pair in range(PAIRS):
        lanes = pair_lanes(pair)
        queries = q_ref[:, lanes].astype(f32) * (1.0 / math.sqrt(HEAD))
        grads = g_ref[:, lanes].astype(f32)
        for half in range(2):
            mine = (lane >= 64) if half else (lane < 64)
            qm[2 * pair + half] = jnp.where(mine, queries, 0.0).astype(bf16)
            gm[2 * pair + half] = jnp.where(mine, grads, 0.0).astype(bf16)

    for level in range(1, LEVELS + 1):
        count = level_rows(level)
        base = contribution_base(level)
        width = contribution_width(level)
        r = lax.broadcasted_iota(jnp.int32, (BLOCK, width), 0)
        c = lax.broadcasted_iota(jnp.int32, (BLOCK, width), 1)
        upsample[:, base : base + width] = jnp.where(
            lax.rem(c, count) == r // 2**level, 0.5**level, 0.0
        ).astype(bf16)

    def forward(part, load, size, valid, offset, unit):
        blocks_in = len(valid)
        step = size // blocks_in
        for pair in pairs_of(part):
            lanes = pair_lanes(pair)
            keys, values = load(0, lanes), load(1, lanes)
            outs = []
            for half in range(2):
                head = 2 * pair + half
                scores = dot_nt(keys, qm[head])
                blocks = [scores[i * step : (i + 1) * step] for i in range(blocks_in)]
                high = None
                for block, flag in zip(blocks, valid):
                    peak = jnp.max(block, axis=0, keepdims=True)
                    if flag is not None:
                        peak = jnp.where(flag, peak, -OUTSIDE)
                    high = peak if high is None else jnp.maximum(high, peak)
                weights, sums = [], None
                for block, flag in zip(blocks, valid):
                    shift = high if flag is None else jnp.where(flag, high, OUTSIDE)
                    weight = jnp.exp(block - shift)
                    added = jnp.sum(weight, axis=0, keepdims=True)
                    sums = added if sums is None else sums + added
                    weights.append(weight.astype(bf16))
                weight = weights[0] if blocks_in == 1 else jnp.concatenate(weights, axis=0)
                prob[head, offset : offset + size] = weight
                outs.append(dot_tn(weight, values))
                top[unit, head] = high
                total[unit, head] = sums
            out_part[unit, pair] = jnp.where(first_head, outs[0], outs[1])

    def near_load(slot):
        return lambda kv, lanes: near[slot, kv, :, lanes]

    def piece_load(level):
        return lambda kv, lanes: jnp.concatenate(
            [pieces[level - 1, slot, kv, :, lanes] for slot in range(3)], axis=0
        )

    far_valid = jnp.logical_or(
        jnp.logical_and(core == 0, me >= 1), jnp.logical_and(core == 1, me < n - 1)
    )
    level_valid = {}
    for level in range(1, LEVELS + 1):
        size = group_size(level)
        group, count = me // size, n // size
        odd = lax.rem(group, 2)
        third = group + 3 - 6 * odd
        level_valid[level] = [
            group >= 2,
            group + 2 < count,
            jnp.logical_and(third >= 0, third < count),
        ]

    def pass_on(part, level):
        lanes = group_lanes(part)
        for slot in range(3):
            at = 3 * (level - 1) + slot
            ref = pieces.at[level - 1, slot, :, half_rows, lanes]
            arrived(ref, plane_recv.at[part, at])
            remote(ref, ref, twin_send.at[part, at], twin_recv.at[part, at], twin)

    def pass_on_first(part):
        lanes = group_lanes(part)
        ref = pieces.at[0, core, :, :, lanes]
        arrived(ref, plane_recv.at[part, 0])
        remote(
            ref, pieces.at[0, 2, :, :, lanes],
            twin_send.at[part, 0], twin_recv.at[part, 0], twin,
        )

    def forward_level(part, level):
        lanes = group_lanes(part)
        if level == 1:
            arrived(pieces.at[0, 2, :, :, lanes], twin_recv.at[part, 0])
            arrived(pieces.at[0, 1 - core, :, :, lanes], twin_recv.at[part, 1])
        else:
            for slot in range(3):
                arrived(
                    pieces.at[level - 1, slot, :, other_rows, lanes],
                    twin_recv.at[part, 3 * (level - 1) + slot],
                )
        unit = NEAR_UNITS + level - 1
        forward(part, piece_load(level), 384, level_valid[level], unit_offset(unit), unit)

    def forward_own(part):
        forward(part, near_load(OWN), BLOCK, [None], unit_offset(0), 0)

    def forward_twin(part):
        arrived(near.at[twin_slot, :, :, group_lanes(part)], near_recv.at[part, 1])
        forward(part, near_load(twin_slot), BLOCK, [None], unit_offset(1), 1)

    def forward_far(part):
        lanes = group_lanes(part)
        arrived(near.at[far_slot, :, :, lanes], near_recv.at[part, 0])
        for kv in range(2):
            derived[kv, :, lanes] = dot_nn(average[...], near[far_slot, kv, :, lanes]).astype(bf16)
        remote(
            derived.at[:, :, lanes], pieces.at[0, core, :, :, lanes],
            twin_send.at[part, 1], twin_recv.at[part, 1], twin,
        )
        forward(part, near_load(far_slot), BLOCK, [far_valid], unit_offset(2), 2)

    units = range(NEAR_UNITS + LEVELS)
    head_row = lax.broadcasted_iota(jnp.int32, (8, 128), 0)
    head_lane = lax.broadcasted_iota(jnp.int32, (8, 128), 1) // 64
    head_sum = jnp.where(head_row == head_lane, 1.0, 0.0).astype(bf16)

    def finish(part):
        for pair in pairs_of(part):
            lanes = pair_lanes(pair)
            rows = []
            for half in range(2):
                head = 2 * pair + half
                high = functools.reduce(jnp.maximum, [top[unit, head] for unit in units])
                fades = [jnp.exp(top[unit, head] - high) for unit in units]
                scale = 1.0 / sum(fade * total[unit, head] for unit, fade in zip(units, fades))
                for unit, fade in zip(units, fades):
                    factor[unit, head] = fade * scale
                    rows.append(fade * scale)
            rows += [jnp.zeros_like(rows[0])] * (16 - len(rows))
            columns = jnp.transpose(jnp.concatenate(rows, axis=0))
            out = None
            for unit in units:
                second = len(units) + unit
                both = jnp.where(
                    first_head, columns[:, unit : unit + 1], columns[:, second : second + 1]
                )
                added = out_part[unit, pair] * both
                out = added if out is None else out + added
            att_ref[:, lanes] = out.astype(bf16)
            product = out * g_ref[:, lanes].astype(f32)
            coarse = product.astype(bf16)
            rest = (product - coarse.astype(f32)).astype(bf16)
            deltas = dot_nt(head_sum, coarse) + dot_nt(head_sum, rest)
            for half in range(2):
                delta[2 * pair + half] = deltas[half : half + 1]
                dq_part[2 * pair + half] = jnp.zeros((BLOCK, 128), f32)

    def backward(part, load, size, offset, unit, store):
        for pair in pairs_of(part):
            lanes = pair_lanes(pair)
            keys, values = load(0, lanes), load(1, lanes)
            key_part, value_part = None, None
            for half in range(2):
                head = 2 * pair + half
                wide = prob[head, offset : offset + size].astype(f32) * factor[unit, head]
                dscore = (wide * (dot_nt(values, gm[head]) - delta[head])).astype(bf16)
                key_new = dot_nn(dscore, qm[head])
                value_new = dot_nn(wide.astype(bf16), gm[head])
                key_part = key_new if key_part is None else key_part + key_new
                value_part = value_new if value_part is None else value_part + value_new
                dq_part[head] += dot_tn(dscore, keys)
            store(lanes, key_part, value_part)

    def near_store(slot):
        def store(lanes, key_part, value_part):
            near_grad[slot, 0, :, lanes] = key_part.astype(bf16)
            near_grad[slot, 1, :, lanes] = value_part.astype(bf16)
        return store

    def own_store(lanes, key_part, value_part):
        own_grad[0, :, lanes] = key_part
        own_grad[1, :, lanes] = value_part

    def piece_store(level):
        def store(lanes, key_part, value_part):
            for slot in range(3):
                at = slice(slot * 128, slot * 128 + 128)
                piece_grad[level - 1, slot, 0, :, lanes] = key_part[at].astype(bf16)
                piece_grad[level - 1, slot, 1, :, lanes] = value_part[at].astype(bf16)
        return store

    def backward_level(part, level):
        unit = NEAR_UNITS + level - 1
        backward(part, piece_load(level), 384, unit_offset(unit), unit, piece_store(level))
        lanes = group_lanes(part)
        if level == 1:
            for i, slot in enumerate((2, 1 - core)):
                remote(
                    piece_grad.at[0, slot, :, :, lanes], twin_first.at[i, :, :, lanes],
                    gtwin_send.at[part, i], gtwin_recv.at[part, i], twin,
                )
            return
        for slot in range(3):
            at = 3 * (level - 1) + slot
            remote(
                piece_grad.at[level - 1, slot, :, other_rows, lanes],
                twin_grad.at[level - 2, slot, :, :, lanes],
                gtwin_send.at[part, at], gtwin_recv.at[part, at], twin,
            )

    def grads_to_owners(part, level):
        lanes = group_lanes(part)
        rows = level_rows(level)
        for slot in range(3):
            arrived(
                twin_grad.at[level - 2, slot, :, :, lanes],
                gtwin_recv.at[part, 3 * (level - 1) + slot],
            )
            for kv in range(2):
                piece_grad[level - 1, slot, kv, half_rows, lanes] = (
                    piece_grad[level - 1, slot, kv, half_rows, lanes].astype(f32)
                    + twin_grad[level - 2, slot, kv, :, lanes].astype(f32)
                ).astype(bf16)
        targets = group_targets(level)
        place = {4: 1, 3: 4, 2: 10}[level]
        for slot in range(3):
            for chip in range(plane_chips(level)):
                if level == 4:
                    remote(
                        piece_grad.at[3, slot, :, half_rows, lanes],
                        row_grads.at[slot, :, :, lanes],
                        gplane_send.at[part, place], gplane_recv.at[part, 3 + slot],
                        plane_target(4, targets[slot], 0),
                    )
                else:
                    source = pl.multiple_of(core * 64 + chip * rows, 16)
                    base = contribution_base(level) + slot * 64
                    target = pl.multiple_of(base + chip_place(level) * rows, 16)
                    remote(
                        piece_grad.at[level - 1, slot, :, pl.ds(source, rows), lanes],
                        coarse_in.at[:, pl.ds(target, rows), lanes],
                        gplane_send.at[part, place], gplane_recv.at[part, level - 1],
                        plane_target(level, targets[slot], chip),
                    )
                place += 1

    def first_to_owner(part):
        lanes = group_lanes(part)
        arrived(twin_first.at[0, :, :, lanes], gtwin_recv.at[part, 0])
        for kv in range(2):
            piece_grad[0, core, kv, :, lanes] = (
                piece_grad[0, core, kv, :, lanes].astype(f32)
                + twin_first[0, kv, :, lanes].astype(f32)
            ).astype(bf16)
        remote(
            piece_grad.at[0, core, :, :, lanes], coarse_in.at[:, pl.ds(0, 128), lanes],
            gplane_send.at[part, 0], gplane_recv.at[part, 0], wrapped(me - 2 + 4 * core),
        )

    def backward_far(part):
        lanes = group_lanes(part)
        backward(part, near_load(far_slot), BLOCK, unit_offset(2), 2, near_store(1))
        arrived(twin_first.at[1, :, :, lanes], gtwin_recv.at[part, 1])
        for kv in range(2):
            near_grad[1, kv, :, lanes] = (
                near_grad[1, kv, :, lanes].astype(f32)
                + dot_nn(upsample[:, :128], twin_first[1, kv, :, lanes])
            ).astype(bf16)
        remote(
            near_grad.at[1, :, :, lanes], near_in.at[1, :, :, lanes],
            gnear_send.at[part, 1], gnear_recv.at[part, 1], far_device,
        )

    def backward_twin(part):
        lanes = group_lanes(part)
        backward(part, near_load(twin_slot), BLOCK, unit_offset(1), 1, near_store(0))
        remote(
            near_grad.at[0, :, :, lanes], near_in.at[0, :, :, lanes],
            gnear_send.at[part, 0], gnear_recv.at[part, 0], twin,
        )

    def backward_own(part):
        backward(part, near_load(OWN), BLOCK, unit_offset(0), 0, own_store)
        for pair in pairs_of(part):
            both = jnp.where(first_head, dq_part[2 * pair], dq_part[2 * pair + 1])
            dq_ref[:, pair_lanes(pair)] = (both * (1.0 / math.sqrt(HEAD))).astype(bf16)

    def row_to_owners(part):
        lanes = group_lanes(part)
        for slot in range(3):
            arrived(row_grads.at[slot, :, :, lanes], gplane_recv.at[part, 3 + slot])
        for kv in range(2):
            added = row_grads[0, kv, :, lanes].astype(f32) + row_grads[1, kv, :, lanes].astype(f32)
            row_sum[kv, :, lanes] = (added + row_grads[2, kv, :, lanes].astype(f32)).astype(bf16)
        target = pl.ds(pl.multiple_of(contribution_base(4) + row_place * 16, 16), 16)
        for kv in range(2):
            coarse_in[kv, target, lanes] = row_sum[kv, own_row, lanes]
        for step in (1, 3, 2):
            place, device = row_partner(step)
            remote(
                row_sum.at[:, pl.ds(pl.multiple_of(place * 16, 16), 16), lanes],
                coarse_in.at[:, target, lanes],
                grow_send.at[part, step - 1], grow_recv.at[part, step - 1], device,
            )

    def write(part):
        lanes = group_lanes(part)
        arrived(near_in.at[0, :, :, lanes], gnear_recv.at[part, 0])
        arrived(near_in.at[1, :, :, lanes], gnear_recv.at[part, 1])
        for level in range(1, LEVELS):
            base, width = contribution_base(level), contribution_width(level)
            arrived(coarse_in.at[:, pl.ds(base, width), lanes], gplane_recv.at[part, level - 1])
        for step in (1, 3, 2):
            base = contribution_base(4) + lax.rem(row_place + 4 - step, 4) * 16
            arrived(
                coarse_in.at[:, pl.ds(pl.multiple_of(base, 16), 16), lanes],
                grow_recv.at[part, step - 1],
            )
        for kv, out_ref in ((0, dk_ref), (1, dv_ref)):
            out = own_grad[kv, :, lanes] + near_in[0, kv, :, lanes].astype(f32)
            out = out + near_in[1, kv, :, lanes].astype(f32)
            out = out + dot_nn(upsample[...], coarse_in[kv, :, lanes])
            out_ref[:, lanes] = out.astype(bf16)

    forward_own(0)
    forward_own(1)
    forward_twin(0)
    pass_on(0, 3)
    pass_on(0, 2)
    forward_level(0, 3)
    pass_on(0, 4)
    pass_on_first(0)
    forward_level(0, 2)
    forward_far(0)
    forward_level(0, 4)
    forward_twin(1)
    forward_level(0, 1)
    finish(0)
    backward_level(0, 1)
    backward_level(0, 4)
    first_to_owner(0)
    backward_far(0)
    grads_to_owners(0, 4)
    pass_on(1, 3)
    backward_level(0, 3)
    pass_on(1, 2)
    backward_level(0, 2)
    grads_to_owners(0, 3)
    pass_on(1, 4)
    pass_on_first(1)
    backward_twin(0)
    grads_to_owners(0, 2)
    forward_level(1, 3)
    forward_level(1, 2)
    forward_level(1, 4)
    forward_far(1)
    backward_own(0)
    row_to_owners(0)
    forward_level(1, 1)
    finish(1)
    backward_level(1, 1)
    backward_level(1, 4)
    first_to_owner(1)
    backward_far(1)
    grads_to_owners(1, 4)
    backward_level(1, 3)
    backward_level(1, 2)
    grads_to_owners(1, 3)
    backward_twin(1)
    grads_to_owners(1, 2)
    backward_own(1)
    write(0)
    row_to_owners(1)
    write(1)
    for copy in started:
        copy.wait_send()


def hand_over(*refs):
    sources, targets, (held, in_sem, out_sem) = refs[:4], refs[4:8], refs[8:]
    inward = [
        pltpu.make_async_copy(source, held.at[i], in_sem.at[i]) for i, source in enumerate(sources)
    ]
    outward = [
        pltpu.make_async_copy(held.at[i], target, out_sem.at[i]) for i, target in enumerate(targets)
    ]
    for copy in inward:
        copy.start()
    for first, second in zip(inward, outward):
        first.wait()
        second.start()
    for copy in outward:
        copy.wait()


def on_device(device_count, sub_count, queries, keys, values, cotangent):
    vmem = pl.BlockSpec(memory_space=pltpu.VMEM)
    dma = pltpu.SemaphoreType.DMA
    rows = (BLOCK, FEATURES)
    plane_messages = 1 + 3 + 6 + 3
    scratch = [
        pltpu.VMEM((3, 2) + rows, bf16),
        pltpu.VMEM((2, 128, FEATURES), bf16),
        pltpu.VMEM((2, 64, FEATURES), bf16),
        pltpu.VMEM((2, 32, FEATURES), bf16),
        pltpu.VMEM((2, 16, FEATURES), bf16),
        pltpu.VMEM((LEVELS, 3, 2, 128, FEATURES), bf16),
        pltpu.VMEM((HEADS, BLOCK, 128), bf16),
        pltpu.VMEM((HEADS, BLOCK, 128), bf16),
        pltpu.VMEM((HEADS, KEYS, BLOCK), bf16),
        pltpu.VMEM((NEAR_UNITS + LEVELS, HEADS, 1, BLOCK), f32),
        pltpu.VMEM((NEAR_UNITS + LEVELS, HEADS, 1, BLOCK), f32),
        pltpu.VMEM((NEAR_UNITS + LEVELS, PAIRS, BLOCK, 128), f32),
        pltpu.VMEM((HEADS, BLOCK, 128), f32),
        pltpu.VMEM((NEAR_UNITS + LEVELS, HEADS, 1, BLOCK), f32),
        pltpu.VMEM((HEADS, 1, BLOCK), f32),
        pltpu.VMEM((BLOCK, CONTRIBUTIONS), bf16),
        pltpu.VMEM((128, BLOCK), bf16),
        pltpu.VMEM((2, 2) + rows, bf16),
        pltpu.VMEM((2,) + rows, f32),
        pltpu.VMEM((LEVELS, 3, 2, 128, FEATURES), bf16),
        pltpu.VMEM((LEVELS - 1, 3, 2, 64, FEATURES), bf16),
        pltpu.VMEM((2, 2, 128, FEATURES), bf16),
        pltpu.VMEM((2, 2) + rows, bf16),
        pltpu.VMEM((2, CONTRIBUTIONS, FEATURES), bf16),
        pltpu.VMEM((2, 64, FEATURES), bf16),
        pltpu.VMEM((3, 2, 64, FEATURES), bf16),
        pltpu.VMEM((2, 64, FEATURES), bf16),
        pltpu.VMEM((2, 128, FEATURES), bf16),
        dma((2, 2)), dma((2, 2)),
        dma((2, plane_messages)), dma((2, 3 * LEVELS)),
        dma((2, 3 * LEVELS)), dma((2, 3 * LEVELS)),
        dma((2, 2)), dma((2, 2)),
        dma((2, plane_messages)), dma((2, LEVELS + 2)),
        dma((2, 3 * LEVELS)), dma((2, 3 * LEVELS)),
        dma((3,)), dma((3,)), dma((2, 3)), dma((2, 3)),
    ]
    results = pl.pallas_call(
        functools.partial(kernel, device_count, sub_count),
        out_shape=[jax.ShapeDtypeStruct(rows, bf16)] * 4,
        in_specs=[vmem] * 4,
        out_specs=[vmem] * 4,
        scratch_shapes=scratch,
        compiler_params=pltpu.CompilerParams(
            collective_id=0, has_side_effects=True, vmem_limit_bytes=56 * 2**20
        ),
        name="hierarchical_attention",
    )(queries, keys, values, cotangent)
    anywhere = pl.BlockSpec(memory_space=pl.ANY)
    return pl.pallas_call(
        hand_over,
        out_shape=[jax.ShapeDtypeStruct(rows, bf16)] * 4,
        in_specs=[anywhere] * 4,
        out_specs=[anywhere] * 4,
        scratch_shapes=[pltpu.VMEM((4,) + rows, bf16), dma((4,)), dma((4,))],
        name="hand_over",
    )(*results)


def solution(mesh):
    spec = P(("seq", "sub"), None)
    device_count = mesh.shape["seq"] * mesh.shape["sub"]
    return jax.shard_map(
        functools.partial(on_device, device_count, mesh.shape["sub"]),
        mesh=mesh,
        in_specs=(spec,) * 4,
        out_specs=(spec,) * 4,
        check_vma=False,
    )
```

```python
import functools
import math

import jax
import jax.numpy as jnp
from jax import lax
from jax.experimental import pallas as pl
from jax.experimental.pallas import tpu as pltpu
from jax.sharding import PartitionSpec as P

MESH = pl.DeviceIdType.MESH
HEADS = 8
HEAD = 64
BLOCK = 256
FEATURES = 512
LEVELS = 4
PAIRS = HEADS // 2
NEAR_UNITS = 3
KEYS = 3 * BLOCK + 3 * LEVELS * 128
CONTRIBUTIONS = 128 + 128 + 192 + 64
OUTSIDE = 1e30
bf16 = jnp.bfloat16
f32 = jnp.float32

OWN, LEFT, RIGHT = 0, 1, 2


def dot_nt(a, b):
    return lax.dot_general(a, b, (((1,), (1,)), ((), ())), preferred_element_type=f32)


def dot_tn(a, b):
    return lax.dot_general(a, b, (((0,), (0,)), ((), ())), preferred_element_type=f32)


def dot_nn(a, b):
    return lax.dot_general(a, b, (((1,), (0,)), ((), ())), preferred_element_type=f32)


def level_rows(level):
    return BLOCK >> level


def unit_offset(unit):
    return unit * BLOCK if unit < NEAR_UNITS else 3 * BLOCK + (unit - NEAR_UNITS) * 384


def contribution_base(level):
    return (0, 128, 256, 448)[level - 1]


def contribution_width(level):
    return (128, 128, 192, 64)[level - 1]


def kernel(
    device_count,
    sub_count,
    q_ref, k_ref, v_ref, g_ref,
    att_ref, dq_ref, dk_ref, dv_ref,
    near, lev1, lev2, lev3, lev4, pieces,
    qm, gm, prob, top, total, out_part, dq_part, factor, delta,
    upsample, average,
    near_grad, own_grad, piece_grad, twin_grad, twin_first, near_in, coarse_in,
    row_keys, row_grads, row_sum, derived, relayed,
    near_send, near_recv, plane_send, plane_recv, twin_send, twin_recv,
    gnear_send, gnear_recv, gplane_send, gplane_recv, gtwin_send, gtwin_recv,
    row_send, row_recv, grow_send, grow_recv,
):
    n = device_count
    me = lax.axis_index("seq") * sub_count + lax.axis_index("sub")
    core = lax.rem(me, 2)
    twin = me + 1 - 2 * core
    levels = [lev1, lev2, lev3, lev4]

    def wrapped(device):
        return lax.rem(device + n, n)

    def mesh_id(device):
        return (device // sub_count, lax.rem(device, sub_count))

    def group_size(level):
        return 2 ** (level - 1)

    def chips(level):
        return max(group_size(level) // 2, 1)

    def chip_place(level):
        return lax.rem(me // 2, chips(level))

    def group_targets(level):
        size = group_size(level)
        group = me // size
        count = n // size
        odd = lax.rem(group, 2)
        third = lax.rem(group + 3 - 6 * odd + count, count)
        below = lax.rem(group - 2 + count, count)
        above = lax.rem(group + 2, count)
        return [below * size, above * size, third * size]

    row_place = lax.rem(me // 2, 4)
    row_start = me - lax.rem(me, 8)

    def plane_chips(level):
        return 1 if level == 4 else chips(level)

    def plane_target(level, start, chip):
        if level == 1:
            return start
        if level == 4:
            return start + lax.rem(me, 8)
        return start + 2 * chip + core

    def row_partner(step):
        place = lax.rem(row_place + step, 4)
        return place, row_start + 2 * place + core

    partners = [twin, wrapped(me - 1 + 2 * core)]
    for level in range(1, LEVELS + 1):
        starts = group_targets(level)[: 2 if level == 1 else 3]
        for start in starts:
            for chip in range(plane_chips(level)):
                partners.append(plane_target(level, start, chip))
    partners += [row_partner(step)[1] for step in (1, 2, 3)]

    barrier = pltpu.get_barrier_semaphore()
    for partner in partners:
        pl.semaphore_signal(barrier, inc=1, device_id=mesh_id(partner), device_id_type=MESH)

    row = lax.broadcasted_iota(jnp.int32, (BLOCK, BLOCK), 0)
    col = lax.broadcasted_iota(jnp.int32, (BLOCK, BLOCK), 1)
    average[...] = jnp.where(row[:128] == col[:128] // 2, 0.5, 0.0).astype(bf16)
    near[OWN, 0] = k_ref[...]
    near[OWN, 1] = v_ref[...]
    for kv in range(2):
        lev1[kv] = dot_nn(average[...], near[OWN, kv]).astype(bf16)
    for level in range(2, LEVELS + 1):
        fine, coarse = levels[level - 2], levels[level - 1]
        rows = level_rows(level)
        for kv in range(2):
            coarse[kv] = dot_nn(average[:rows, : 2 * rows], fine[kv]).astype(bf16)
    own_row = pl.ds(pl.multiple_of(row_place * 16, 16), 16)
    for kv in range(2):
        row_keys[kv, own_row] = lev4[kv]

    pl.semaphore_wait(barrier, len(partners))

    started = []

    def remote(src, dst, send, recv, device):
        copy = pltpu.make_async_remote_copy(
            src_ref=src, dst_ref=dst, send_sem=send, recv_sem=recv,
            device_id=mesh_id(device), device_id_type=MESH,
        )
        copy.start()
        started.append(copy)

    def arrived(ref, sem):
        pltpu.make_async_copy(ref, ref, sem).wait()

    def group_lanes(part):
        return pl.ds(part * 256, 256)

    for step in (1, 3, 2):
        remote(
            lev4, row_keys.at[:, own_row], row_send.at[step - 1], row_recv.at[step - 1],
            row_partner(step)[1],
        )
    far_slot = LEFT + core
    twin_slot = RIGHT - core
    far_device = wrapped(me - 1 + 2 * core)
    half_rows = pl.ds(pl.multiple_of(core * 64, 64), 64)
    other_rows = pl.ds(pl.multiple_of(64 - core * 64, 64), 64)

    chip_odd = lax.rem(me // 2, 2)
    beside = wrapped(me + 2 - 4 * chip_odd)
    two_off = wrapped(me - 4 + 8 * chip_odd)
    two_back = wrapped(me + 4 - 8 * chip_odd)

    def send_keys(part):
        lanes = group_lanes(part)
        block = near.at[OWN, :, :, lanes]
        remote(
            block, near.at[RIGHT - core, :, :, lanes],
            near_send.at[part, 0], near_recv.at[part, 0], far_device,
        )
        remote(
            block, near.at[LEFT + core, :, :, lanes],
            near_send.at[part, 1], near_recv.at[part, 1], twin,
        )
        place = 0
        rows = level_rows(2)
        offset = pl.multiple_of(core * 64, 64)
        third = group_targets(2)[2] + core
        for slot, device in ((2, third), (1 - chip_odd, two_off)):
            remote(
                lev2.at[:, :, lanes], pieces.at[1, slot, :, pl.ds(offset, rows), lanes],
                plane_send.at[part, place], plane_recv.at[part, 3 + slot], device,
            )
            place += 1
        rows = level_rows(3)
        targets = group_targets(3)
        for slot, start in ((1, targets[0]), (0, targets[1]), (2, targets[2])):
            for chip in range(chips(3)):
                offset = pl.multiple_of(core * 64 + chip_place(3) * rows, 16)
                remote(
                    lev3.at[:, :, lanes],
                    pieces.at[2, slot, :, pl.ds(offset, rows), lanes],
                    plane_send.at[part, place], plane_recv.at[part, 6 + slot],
                    plane_target(3, start, chip),
                )
                place += 1
        remote(
            lev1.at[:, :, lanes], pieces.at[0, core, :, :, lanes],
            plane_send.at[part, place], plane_recv.at[part, 0], wrapped(me + 2 - 4 * core),
        )

    def send_row(part):
        lanes = group_lanes(part)
        targets = group_targets(4)
        for slot, start in ((1, targets[0]), (0, targets[1]), (2, targets[2])):
            remote(
                row_keys.at[:, :, lanes], pieces.at[3, slot, :, half_rows, lanes],
                plane_send.at[part, 10 + slot], plane_recv.at[part, 9 + slot],
                plane_target(4, start, 0),
            )

    send_keys(0)
    for step in (1, 3, 2):
        from_place = lax.rem(row_place + 4 - step, 4)
        arrived(
            row_keys.at[:, pl.ds(pl.multiple_of(from_place * 16, 16), 16)], row_recv.at[step - 1]
        )
    send_row(0)
    send_row(1)
    send_keys(1)

    lane = lax.broadcasted_iota(jnp.int32, (BLOCK, 128), 1)
    first_head = lane < 64

    def pairs_of(part):
        return range(2 * part, 2 * part + 2)

    def pair_lanes(pair):
        return slice(pair * 128, pair * 128 + 128)

    for pair in range(PAIRS):
        lanes = pair_lanes(pair)
        queries = q_ref[:, lanes].astype(f32) * (1.0 / math.sqrt(HEAD))
        grads = g_ref[:, lanes].astype(f32)
        for half in range(2):
            mine = (lane >= 64) if half else (lane < 64)
            qm[2 * pair + half] = jnp.where(mine, queries, 0.0).astype(bf16)
            gm[2 * pair + half] = jnp.where(mine, grads, 0.0).astype(bf16)

    for level in range(1, LEVELS + 1):
        count = level_rows(level)
        base = contribution_base(level)
        width = contribution_width(level)
        r = lax.broadcasted_iota(jnp.int32, (BLOCK, width), 0)
        c = lax.broadcasted_iota(jnp.int32, (BLOCK, width), 1)
        upsample[:, base : base + width] = jnp.where(
            lax.rem(c, count) == r // 2**level, 0.5**level, 0.0
        ).astype(bf16)

    def forward(part, load, size, valid, offset, unit):
        blocks_in = len(valid)
        step = size // blocks_in
        for pair in pairs_of(part):
            lanes = pair_lanes(pair)
            keys, values = load(0, lanes), load(1, lanes)
            outs = []
            for half in range(2):
                head = 2 * pair + half
                scores = dot_nt(keys, qm[head])
                blocks = [scores[i * step : (i + 1) * step] for i in range(blocks_in)]
                high = None
                for block, flag in zip(blocks, valid):
                    peak = jnp.max(block, axis=0, keepdims=True)
                    if flag is not None:
                        peak = jnp.where(flag, peak, -OUTSIDE)
                    high = peak if high is None else jnp.maximum(high, peak)
                weights, sums = [], None
                for block, flag in zip(blocks, valid):
                    shift = high if flag is None else jnp.where(flag, high, OUTSIDE)
                    weight = jnp.exp(block - shift)
                    added = jnp.sum(weight, axis=0, keepdims=True)
                    sums = added if sums is None else sums + added
                    weights.append(weight.astype(bf16))
                weight = weights[0] if blocks_in == 1 else jnp.concatenate(weights, axis=0)
                prob[head, offset : offset + size] = weight
                outs.append(dot_tn(weight, values))
                top[unit, head] = high
                total[unit, head] = sums
            out_part[unit, pair] = jnp.where(first_head, outs[0], outs[1])

    def near_load(slot):
        return lambda kv, lanes: near[slot, kv, :, lanes]

    def piece_load(level):
        return lambda kv, lanes: jnp.concatenate(
            [pieces[level - 1, slot, kv, :, lanes] for slot in range(3)], axis=0
        )

    far_valid = jnp.logical_or(
        jnp.logical_and(core == 0, me >= 1), jnp.logical_and(core == 1, me < n - 1)
    )
    level_valid = {}
    for level in range(1, LEVELS + 1):
        size = group_size(level)
        group, count = me // size, n // size
        odd = lax.rem(group, 2)
        third = group + 3 - 6 * odd
        level_valid[level] = [
            group >= 2,
            group + 2 < count,
            jnp.logical_and(third >= 0, third < count),
        ]

    def pass_on(part, level):
        lanes = group_lanes(part)
        for slot in (2, 1 - chip_odd, chip_odd) if level == 2 else range(3):
            at = 3 * (level - 1) + slot
            ref = pieces.at[level - 1, slot, :, half_rows, lanes]
            arrived(ref, plane_recv.at[part, at])
            if level == 2 and isinstance(slot, int):
                remote(
                    ref, pieces.at[1, 1 - chip_odd, :, half_rows, lanes],
                    plane_send.at[part, 9], plane_recv.at[part, 4 - chip_odd], beside,
                )
            remote(ref, ref, twin_send.at[part, at], twin_recv.at[part, at], twin)

    def pass_on_first(part):
        lanes = group_lanes(part)
        ref = pieces.at[0, core, :, :, lanes]
        arrived(ref, plane_recv.at[part, 0])
        remote(
            ref, pieces.at[0, 2, :, :, lanes],
            twin_send.at[part, 0], twin_recv.at[part, 0], twin,
        )

    def forward_level(part, level):
        lanes = group_lanes(part)
        if level == 1:
            arrived(pieces.at[0, 2, :, :, lanes], twin_recv.at[part, 0])
            arrived(pieces.at[0, 1 - core, :, :, lanes], twin_recv.at[part, 1])
        else:
            for slot in range(3):
                arrived(
                    pieces.at[level - 1, slot, :, other_rows, lanes],
                    twin_recv.at[part, 3 * (level - 1) + slot],
                )
        unit = NEAR_UNITS + level - 1
        forward(part, piece_load(level), 384, level_valid[level], unit_offset(unit), unit)

    def forward_own(part):
        forward(part, near_load(OWN), BLOCK, [None], unit_offset(0), 0)

    def forward_twin(part):
        arrived(near.at[twin_slot, :, :, group_lanes(part)], near_recv.at[part, 1])
        forward(part, near_load(twin_slot), BLOCK, [None], unit_offset(1), 1)

    def forward_far(part):
        lanes = group_lanes(part)
        arrived(near.at[far_slot, :, :, lanes], near_recv.at[part, 0])
        for kv in range(2):
            derived[kv, :, lanes] = dot_nn(average[...], near[far_slot, kv, :, lanes]).astype(bf16)
        remote(
            derived.at[:, :, lanes], pieces.at[0, core, :, :, lanes],
            twin_send.at[part, 1], twin_recv.at[part, 1], twin,
        )
        forward(part, near_load(far_slot), BLOCK, [far_valid], unit_offset(2), 2)

    units = range(NEAR_UNITS + LEVELS)
    head_row = lax.broadcasted_iota(jnp.int32, (8, 128), 0)
    head_lane = lax.broadcasted_iota(jnp.int32, (8, 128), 1) // 64
    head_sum = jnp.where(head_row == head_lane, 1.0, 0.0).astype(bf16)

    def finish(part):
        for pair in pairs_of(part):
            lanes = pair_lanes(pair)
            rows = []
            for half in range(2):
                head = 2 * pair + half
                high = functools.reduce(jnp.maximum, [top[unit, head] for unit in units])
                fades = [jnp.exp(top[unit, head] - high) for unit in units]
                scale = 1.0 / sum(fade * total[unit, head] for unit, fade in zip(units, fades))
                for unit, fade in zip(units, fades):
                    factor[unit, head] = fade * scale
                    rows.append(fade * scale)
            rows += [jnp.zeros_like(rows[0])] * (16 - len(rows))
            columns = jnp.transpose(jnp.concatenate(rows, axis=0))
            out = None
            for unit in units:
                second = len(units) + unit
                both = jnp.where(
                    first_head, columns[:, unit : unit + 1], columns[:, second : second + 1]
                )
                added = out_part[unit, pair] * both
                out = added if out is None else out + added
            att_ref[:, lanes] = out.astype(bf16)
            product = out * g_ref[:, lanes].astype(f32)
            coarse = product.astype(bf16)
            rest = (product - coarse.astype(f32)).astype(bf16)
            deltas = dot_nt(head_sum, coarse) + dot_nt(head_sum, rest)
            for half in range(2):
                delta[2 * pair + half] = deltas[half : half + 1]
                dq_part[2 * pair + half] = jnp.zeros((BLOCK, 128), f32)

    def backward(part, load, size, offset, unit, store):
        for pair in pairs_of(part):
            lanes = pair_lanes(pair)
            keys, values = load(0, lanes), load(1, lanes)
            key_part, value_part = None, None
            for half in range(2):
                head = 2 * pair + half
                wide = prob[head, offset : offset + size].astype(f32) * factor[unit, head]
                dscore = (wide * (dot_nt(values, gm[head]) - delta[head])).astype(bf16)
                key_new = dot_nn(dscore, qm[head])
                value_new = dot_nn(wide.astype(bf16), gm[head])
                key_part = key_new if key_part is None else key_part + key_new
                value_part = value_new if value_part is None else value_part + value_new
                dq_part[head] += dot_tn(dscore, keys)
            store(lanes, key_part, value_part)

    def near_store(slot):
        def store(lanes, key_part, value_part):
            near_grad[slot, 0, :, lanes] = key_part.astype(bf16)
            near_grad[slot, 1, :, lanes] = value_part.astype(bf16)
        return store

    def own_store(lanes, key_part, value_part):
        own_grad[0, :, lanes] = key_part
        own_grad[1, :, lanes] = value_part

    def piece_store(level):
        def store(lanes, key_part, value_part):
            for slot in range(3):
                at = slice(slot * 128, slot * 128 + 128)
                piece_grad[level - 1, slot, 0, :, lanes] = key_part[at].astype(bf16)
                piece_grad[level - 1, slot, 1, :, lanes] = value_part[at].astype(bf16)
        return store

    def backward_level(part, level):
        unit = NEAR_UNITS + level - 1
        backward(part, piece_load(level), 384, unit_offset(unit), unit, piece_store(level))
        lanes = group_lanes(part)
        if level == 1:
            for i, slot in enumerate((2, 1 - core)):
                remote(
                    piece_grad.at[0, slot, :, :, lanes], twin_first.at[i, :, :, lanes],
                    gtwin_send.at[part, i], gtwin_recv.at[part, i], twin,
                )
            return
        for slot in range(3):
            at = 3 * (level - 1) + slot
            remote(
                piece_grad.at[level - 1, slot, :, other_rows, lanes],
                twin_grad.at[level - 2, slot, :, :, lanes],
                gtwin_send.at[part, at], gtwin_recv.at[part, at], twin,
            )

    def grads_to_owners(part, level):
        lanes = group_lanes(part)
        rows = level_rows(level)
        for slot in range(3):
            arrived(
                twin_grad.at[level - 2, slot, :, :, lanes],
                gtwin_recv.at[part, 3 * (level - 1) + slot],
            )
            for kv in range(2):
                piece_grad[level - 1, slot, kv, half_rows, lanes] = (
                    piece_grad[level - 1, slot, kv, half_rows, lanes].astype(f32)
                    + twin_grad[level - 2, slot, kv, :, lanes].astype(f32)
                ).astype(bf16)
        if level == 2:
            remote(
                piece_grad.at[1, chip_odd, :, half_rows, lanes], relayed.at[:, :, lanes],
                gplane_send.at[part, 10], gplane_recv.at[part, 6], beside,
            )
            remote(
                piece_grad.at[1, 1 - chip_odd, :, half_rows, lanes],
                coarse_in.at[:, pl.ds(contribution_base(2), 64), lanes],
                gplane_send.at[part, 11], gplane_recv.at[part, 1], two_back,
            )
            return
        targets = group_targets(level)
        place = {4: 1, 3: 4}[level]
        for slot in range(3):
            for chip in range(plane_chips(level)):
                if level == 4:
                    remote(
                        piece_grad.at[3, slot, :, half_rows, lanes],
                        row_grads.at[slot, :, :, lanes],
                        gplane_send.at[part, place], gplane_recv.at[part, 3 + slot],
                        plane_target(4, targets[slot], 0),
                    )
                else:
                    source = pl.multiple_of(core * 64 + chip * rows, 16)
                    base = contribution_base(level) + slot * 64
                    target = pl.multiple_of(base + chip_place(level) * rows, 16)
                    remote(
                        piece_grad.at[level - 1, slot, :, pl.ds(source, rows), lanes],
                        coarse_in.at[:, pl.ds(target, rows), lanes],
                        gplane_send.at[part, place], gplane_recv.at[part, level - 1],
                        plane_target(level, targets[slot], chip),
                    )
                place += 1

    def relay_to_owner(part):
        lanes = group_lanes(part)
        arrived(relayed.at[:, :, lanes], gplane_recv.at[part, 6])
        for kv in range(2):
            piece_grad[1, 2, kv, half_rows, lanes] = (
                piece_grad[1, 2, kv, half_rows, lanes].astype(f32)
                + relayed[kv, :, lanes].astype(f32)
            ).astype(bf16)
        remote(
            piece_grad.at[1, 2, :, half_rows, lanes],
            coarse_in.at[:, pl.ds(contribution_base(2) + 64, 64), lanes],
            gplane_send.at[part, 12], gplane_recv.at[part, 7], group_targets(2)[2] + core,
        )

    def first_to_owner(part):
        lanes = group_lanes(part)
        arrived(twin_first.at[0, :, :, lanes], gtwin_recv.at[part, 0])
        for kv in range(2):
            piece_grad[0, core, kv, :, lanes] = (
                piece_grad[0, core, kv, :, lanes].astype(f32)
                + twin_first[0, kv, :, lanes].astype(f32)
            ).astype(bf16)
        remote(
            piece_grad.at[0, core, :, :, lanes], coarse_in.at[:, pl.ds(0, 128), lanes],
            gplane_send.at[part, 0], gplane_recv.at[part, 0], wrapped(me - 2 + 4 * core),
        )

    def backward_far(part):
        lanes = group_lanes(part)
        backward(part, near_load(far_slot), BLOCK, unit_offset(2), 2, near_store(1))
        arrived(twin_first.at[1, :, :, lanes], gtwin_recv.at[part, 1])
        for kv in range(2):
            near_grad[1, kv, :, lanes] = (
                near_grad[1, kv, :, lanes].astype(f32)
                + dot_nn(upsample[:, :128], twin_first[1, kv, :, lanes])
            ).astype(bf16)
        remote(
            near_grad.at[1, :, :, lanes], near_in.at[1, :, :, lanes],
            gnear_send.at[part, 1], gnear_recv.at[part, 1], far_device,
        )

    def backward_twin(part):
        lanes = group_lanes(part)
        backward(part, near_load(twin_slot), BLOCK, unit_offset(1), 1, near_store(0))
        remote(
            near_grad.at[0, :, :, lanes], near_in.at[0, :, :, lanes],
            gnear_send.at[part, 0], gnear_recv.at[part, 0], twin,
        )

    def backward_own(part):
        backward(part, near_load(OWN), BLOCK, unit_offset(0), 0, own_store)
        for pair in pairs_of(part):
            both = jnp.where(first_head, dq_part[2 * pair], dq_part[2 * pair + 1])
            dq_ref[:, pair_lanes(pair)] = (both * (1.0 / math.sqrt(HEAD))).astype(bf16)

    def row_to_owners(part):
        lanes = group_lanes(part)
        for slot in range(3):
            arrived(row_grads.at[slot, :, :, lanes], gplane_recv.at[part, 3 + slot])
        for kv in range(2):
            added = row_grads[0, kv, :, lanes].astype(f32) + row_grads[1, kv, :, lanes].astype(f32)
            row_sum[kv, :, lanes] = (added + row_grads[2, kv, :, lanes].astype(f32)).astype(bf16)
        target = pl.ds(pl.multiple_of(contribution_base(4) + row_place * 16, 16), 16)
        for kv in range(2):
            coarse_in[kv, target, lanes] = row_sum[kv, own_row, lanes]
        for step in (1, 3, 2):
            place, device = row_partner(step)
            remote(
                row_sum.at[:, pl.ds(pl.multiple_of(place * 16, 16), 16), lanes],
                coarse_in.at[:, target, lanes],
                grow_send.at[part, step - 1], grow_recv.at[part, step - 1], device,
            )

    def write(part):
        lanes = group_lanes(part)
        arrived(near_in.at[0, :, :, lanes], gnear_recv.at[part, 0])
        arrived(near_in.at[1, :, :, lanes], gnear_recv.at[part, 1])
        for base, width, sem in ((0, 128, 0), (128, 64, 1), (192, 64, 7), (256, 192, 2)):
            arrived(coarse_in.at[:, pl.ds(base, width), lanes], gplane_recv.at[part, sem])
        for step in (1, 3, 2):
            base = contribution_base(4) + lax.rem(row_place + 4 - step, 4) * 16
            arrived(
                coarse_in.at[:, pl.ds(pl.multiple_of(base, 16), 16), lanes],
                grow_recv.at[part, step - 1],
            )
        for kv, out_ref in ((0, dk_ref), (1, dv_ref)):
            out = own_grad[kv, :, lanes] + near_in[0, kv, :, lanes].astype(f32)
            out = out + near_in[1, kv, :, lanes].astype(f32)
            out = out + dot_nn(upsample[...], coarse_in[kv, :, lanes])
            out_ref[:, lanes] = out.astype(bf16)

    forward_own(0)
    forward_own(1)
    forward_twin(0)
    pass_on(0, 3)
    pass_on(0, 2)
    forward_level(0, 3)
    pass_on(0, 4)
    pass_on_first(0)
    forward_level(0, 2)
    forward_far(0)
    forward_level(0, 4)
    forward_twin(1)
    forward_level(0, 1)
    finish(0)
    backward_level(0, 1)
    backward_level(0, 4)
    first_to_owner(0)
    backward_far(0)
    grads_to_owners(0, 4)
    backward_level(0, 2)
    backward_level(0, 3)
    grads_to_owners(0, 2)
    pass_on(1, 3)
    pass_on(1, 2)
    backward_twin(0)
    grads_to_owners(0, 3)
    relay_to_owner(0)
    pass_on(1, 4)
    pass_on_first(1)
    forward_level(1, 3)
    forward_level(1, 2)
    forward_level(1, 4)
    forward_far(1)
    backward_own(0)
    row_to_owners(0)
    forward_level(1, 1)
    finish(1)
    backward_level(1, 1)
    backward_level(1, 4)
    first_to_owner(1)
    backward_far(1)
    grads_to_owners(1, 4)
    backward_level(1, 2)
    backward_level(1, 3)
    grads_to_owners(1, 2)
    backward_twin(1)
    grads_to_owners(1, 3)
    relay_to_owner(1)
    backward_own(1)
    write(0)
    row_to_owners(1)
    write(1)
    for copy in started:
        copy.wait_send()


def hand_over(*refs):
    sources, targets, (held, in_sem, out_sem) = refs[:4], refs[4:8], refs[8:]
    inward = [
        pltpu.make_async_copy(source, held.at[i], in_sem.at[i]) for i, source in enumerate(sources)
    ]
    outward = [
        pltpu.make_async_copy(held.at[i], target, out_sem.at[i]) for i, target in enumerate(targets)
    ]
    for copy in inward:
        copy.start()
    for first, second in zip(inward, outward):
        first.wait()
        second.start()
    for copy in outward:
        copy.wait()


def on_device(device_count, sub_count, queries, keys, values, cotangent):
    vmem = pl.BlockSpec(memory_space=pltpu.VMEM)
    dma = pltpu.SemaphoreType.DMA
    rows = (BLOCK, FEATURES)
    plane_messages = 1 + 3 + 6 + 3
    scratch = [
        pltpu.VMEM((3, 2) + rows, bf16),
        pltpu.VMEM((2, 128, FEATURES), bf16),
        pltpu.VMEM((2, 64, FEATURES), bf16),
        pltpu.VMEM((2, 32, FEATURES), bf16),
        pltpu.VMEM((2, 16, FEATURES), bf16),
        pltpu.VMEM((LEVELS, 3, 2, 128, FEATURES), bf16),
        pltpu.VMEM((HEADS, BLOCK, 128), bf16),
        pltpu.VMEM((HEADS, BLOCK, 128), bf16),
        pltpu.VMEM((HEADS, KEYS, BLOCK), bf16),
        pltpu.VMEM((NEAR_UNITS + LEVELS, HEADS, 1, BLOCK), f32),
        pltpu.VMEM((NEAR_UNITS + LEVELS, HEADS, 1, BLOCK), f32),
        pltpu.VMEM((NEAR_UNITS + LEVELS, PAIRS, BLOCK, 128), f32),
        pltpu.VMEM((HEADS, BLOCK, 128), f32),
        pltpu.VMEM((NEAR_UNITS + LEVELS, HEADS, 1, BLOCK), f32),
        pltpu.VMEM((HEADS, 1, BLOCK), f32),
        pltpu.VMEM((BLOCK, CONTRIBUTIONS), bf16),
        pltpu.VMEM((128, BLOCK), bf16),
        pltpu.VMEM((2, 2) + rows, bf16),
        pltpu.VMEM((2,) + rows, f32),
        pltpu.VMEM((LEVELS, 3, 2, 128, FEATURES), bf16),
        pltpu.VMEM((LEVELS - 1, 3, 2, 64, FEATURES), bf16),
        pltpu.VMEM((2, 2, 128, FEATURES), bf16),
        pltpu.VMEM((2, 2) + rows, bf16),
        pltpu.VMEM((2, CONTRIBUTIONS, FEATURES), bf16),
        pltpu.VMEM((2, 64, FEATURES), bf16),
        pltpu.VMEM((3, 2, 64, FEATURES), bf16),
        pltpu.VMEM((2, 64, FEATURES), bf16),
        pltpu.VMEM((2, 128, FEATURES), bf16),
        pltpu.VMEM((2, 64, FEATURES), bf16),
        dma((2, 2)), dma((2, 2)),
        dma((2, plane_messages)), dma((2, 3 * LEVELS)),
        dma((2, 3 * LEVELS)), dma((2, 3 * LEVELS)),
        dma((2, 2)), dma((2, 2)),
        dma((2, plane_messages)), dma((2, LEVELS + 4)),
        dma((2, 3 * LEVELS)), dma((2, 3 * LEVELS)),
        dma((3,)), dma((3,)), dma((2, 3)), dma((2, 3)),
    ]
    results = pl.pallas_call(
        functools.partial(kernel, device_count, sub_count),
        out_shape=[jax.ShapeDtypeStruct(rows, bf16)] * 4,
        in_specs=[vmem] * 4,
        out_specs=[vmem] * 4,
        scratch_shapes=scratch,
        compiler_params=pltpu.CompilerParams(
            collective_id=0, has_side_effects=True, vmem_limit_bytes=56 * 2**20
        ),
        name="hierarchical_attention",
    )(queries, keys, values, cotangent)
    anywhere = pl.BlockSpec(memory_space=pl.ANY)
    return pl.pallas_call(
        hand_over,
        out_shape=[jax.ShapeDtypeStruct(rows, bf16)] * 4,
        in_specs=[anywhere] * 4,
        out_specs=[anywhere] * 4,
        scratch_shapes=[pltpu.VMEM((4,) + rows, bf16), dma((4,)), dma((4,))],
        name="hand_over",
    )(*results)


def solution(mesh):
    spec = P(("seq", "sub"), None)
    device_count = mesh.shape["seq"] * mesh.shape["sub"]
    return jax.shard_map(
        functools.partial(on_device, device_count, mesh.shape["sub"]),
        mesh=mesh,
        in_specs=(spec,) * 4,
        out_specs=(spec,) * 4,
        check_vma=False,
    )
```

```python
import functools
import math

import jax
import jax.numpy as jnp
from jax import lax
from jax.experimental import pallas as pl
from jax.experimental.pallas import tpu as pltpu
from jax.sharding import PartitionSpec as P

MESH = pl.DeviceIdType.MESH
HEADS = 8
HEAD = 64
BLOCK = 256
FEATURES = 512
LEVELS = 4
PAIRS = HEADS // 2
NEAR_UNITS = 3
KEYS = 3 * BLOCK + 3 * LEVELS * 128
CONTRIBUTIONS = 128 + 2 * 192 + 64
OUTSIDE = 1e30
bf16 = jnp.bfloat16
f32 = jnp.float32

OWN, LEFT, RIGHT = 0, 1, 2


def dot_nt(a, b):
    return lax.dot_general(a, b, (((1,), (1,)), ((), ())), preferred_element_type=f32)


def dot_tn(a, b):
    return lax.dot_general(a, b, (((0,), (0,)), ((), ())), preferred_element_type=f32)


def dot_nn(a, b):
    return lax.dot_general(a, b, (((1,), (0,)), ((), ())), preferred_element_type=f32)


def level_rows(level):
    return BLOCK >> level


def unit_offset(unit):
    return unit * BLOCK if unit < NEAR_UNITS else 3 * BLOCK + (unit - NEAR_UNITS) * 384


def contribution_base(level):
    return (0, 128, 320, 512)[level - 1]


def contribution_width(level):
    return (128, 192, 192, 64)[level - 1]


def kernel(
    device_count,
    sub_count,
    q_ref, k_ref, v_ref, g_ref,
    att_ref, dq_ref, dk_ref, dv_ref,
    near, lev1, lev2, lev3, lev4, pieces,
    qm, gm, prob, top, total, out_part, dq_part, factor, delta,
    upsample, average,
    near_grad, own_grad, piece_grad, twin_grad, twin_first, near_in, coarse_in,
    row_keys, row_grads, row_sum, derived,
    near_send, near_recv, plane_send, plane_recv, twin_send, twin_recv,
    gnear_send, gnear_recv, gplane_send, gplane_recv, gtwin_send, gtwin_recv,
    row_send, row_recv, grow_send, grow_recv,
):
    n = device_count
    me = lax.axis_index("seq") * sub_count + lax.axis_index("sub")
    core = lax.rem(me, 2)
    twin = me + 1 - 2 * core
    levels = [lev1, lev2, lev3, lev4]

    def wrapped(device):
        return lax.rem(device + n, n)

    def mesh_id(device):
        return (device // sub_count, lax.rem(device, sub_count))

    def group_size(level):
        return 2 ** (level - 1)

    def chips(level):
        return max(group_size(level) // 2, 1)

    def chip_place(level):
        return lax.rem(me // 2, chips(level))

    def group_targets(level):
        size = group_size(level)
        group = me // size
        count = n // size
        odd = lax.rem(group, 2)
        third = lax.rem(group + 3 - 6 * odd + count, count)
        below = lax.rem(group - 2 + count, count)
        above = lax.rem(group + 2, count)
        return [below * size, above * size, third * size]

    row_place = lax.rem(me // 2, 4)
    row_start = me - lax.rem(me, 8)

    def plane_chips(level):
        return 1 if level == 4 else chips(level)

    def plane_target(level, start, chip):
        if level == 1:
            return start
        if level == 4:
            return start + lax.rem(me, 8)
        return start + 2 * chip + core

    def row_partner(step):
        place = lax.rem(row_place + step, 4)
        return place, row_start + 2 * place + core

    partners = [twin, wrapped(me - 1 + 2 * core)]
    for level in range(1, LEVELS + 1):
        starts = group_targets(level)[: 2 if level == 1 else 3]
        for start in starts:
            for chip in range(plane_chips(level)):
                partners.append(plane_target(level, start, chip))
    partners += [row_partner(step)[1] for step in (1, 2, 3)]

    barrier = pltpu.get_barrier_semaphore()
    for partner in partners:
        pl.semaphore_signal(barrier, inc=1, device_id=mesh_id(partner), device_id_type=MESH)

    row = lax.broadcasted_iota(jnp.int32, (BLOCK, BLOCK), 0)
    col = lax.broadcasted_iota(jnp.int32, (BLOCK, BLOCK), 1)
    average[...] = jnp.where(row[:128] == col[:128] // 2, 0.5, 0.0).astype(bf16)
    near[OWN, 0] = k_ref[...]
    near[OWN, 1] = v_ref[...]
    for kv in range(2):
        lev1[kv] = dot_nn(average[...], near[OWN, kv]).astype(bf16)
    for level in range(2, LEVELS + 1):
        fine, coarse = levels[level - 2], levels[level - 1]
        rows = level_rows(level)
        for kv in range(2):
            coarse[kv] = dot_nn(average[:rows, : 2 * rows], fine[kv]).astype(bf16)
    own_row = pl.ds(pl.multiple_of(row_place * 16, 16), 16)
    for kv in range(2):
        row_keys[kv, own_row] = lev4[kv]

    pl.semaphore_wait(barrier, len(partners))

    started = []

    def remote(src, dst, send, recv, device):
        copy = pltpu.make_async_remote_copy(
            src_ref=src, dst_ref=dst, send_sem=send, recv_sem=recv,
            device_id=mesh_id(device), device_id_type=MESH,
        )
        copy.start()
        started.append(copy)

    def arrived(ref, sem):
        pltpu.make_async_copy(ref, ref, sem).wait()

    def group_lanes(part):
        return pl.ds(384, 128) if part else pl.ds(0, 384)

    for step in (1, 3, 2):
        remote(
            lev4, row_keys.at[:, own_row], row_send.at[step - 1], row_recv.at[step - 1],
            row_partner(step)[1],
        )
    far_slot = LEFT + core
    twin_slot = RIGHT - core
    far_device = wrapped(me - 1 + 2 * core)
    half_rows = pl.ds(pl.multiple_of(core * 64, 64), 64)
    other_rows = pl.ds(pl.multiple_of(64 - core * 64, 64), 64)

    def send_keys(part):
        lanes = group_lanes(part)
        block = near.at[OWN, :, :, lanes]
        remote(
            block, near.at[RIGHT - core, :, :, lanes],
            near_send.at[part, 0], near_recv.at[part, 0], far_device,
        )
        remote(
            block, near.at[LEFT + core, :, :, lanes],
            near_send.at[part, 1], near_recv.at[part, 1], twin,
        )
        place = 0
        for level in (3, 2):
            rows = level_rows(level)
            targets = group_targets(level)
            for slot, start in ((1, targets[0]), (0, targets[1]), (2, targets[2])):
                for chip in range(chips(level)):
                    offset = pl.multiple_of(core * 64 + chip_place(level) * rows, 16)
                    remote(
                        levels[level - 1].at[:, :, lanes],
                        pieces.at[level - 1, slot, :, pl.ds(offset, rows), lanes],
                        plane_send.at[part, place],
                        plane_recv.at[part, 3 * (level - 1) + slot],
                        plane_target(level, start, chip),
                    )
                    place += 1
        remote(
            lev1.at[:, :, lanes], pieces.at[0, core, :, :, lanes],
            plane_send.at[part, place], plane_recv.at[part, 0], wrapped(me + 2 - 4 * core),
        )

    def send_row(part):
        lanes = group_lanes(part)
        targets = group_targets(4)
        for slot, start in ((1, targets[0]), (0, targets[1]), (2, targets[2])):
            remote(
                row_keys.at[:, :, lanes], pieces.at[3, slot, :, half_rows, lanes],
                plane_send.at[part, 10 + slot], plane_recv.at[part, 9 + slot],
                plane_target(4, start, 0),
            )

    send_keys(0)
    for step in (1, 3, 2):
        from_place = lax.rem(row_place + 4 - step, 4)
        arrived(
            row_keys.at[:, pl.ds(pl.multiple_of(from_place * 16, 16), 16)], row_recv.at[step - 1]
        )
    send_row(0)
    send_row(1)
    send_keys(1)

    lane = lax.broadcasted_iota(jnp.int32, (BLOCK, 128), 1)
    first_head = lane < 64

    def pairs_of(part):
        return range(3, 4) if part else range(3)

    def pair_lanes(pair):
        return slice(pair * 128, pair * 128 + 128)

    for pair in range(PAIRS):
        lanes = pair_lanes(pair)
        queries = q_ref[:, lanes].astype(f32) * (1.0 / math.sqrt(HEAD))
        grads = g_ref[:, lanes].astype(f32)
        for half in range(2):
            mine = (lane >= 64) if half else (lane < 64)
            qm[2 * pair + half] = jnp.where(mine, queries, 0.0).astype(bf16)
            gm[2 * pair + half] = jnp.where(mine, grads, 0.0).astype(bf16)

    for level in range(1, LEVELS + 1):
        count = level_rows(level)
        base = contribution_base(level)
        width = contribution_width(level)
        r = lax.broadcasted_iota(jnp.int32, (BLOCK, width), 0)
        c = lax.broadcasted_iota(jnp.int32, (BLOCK, width), 1)
        upsample[:, base : base + width] = jnp.where(
            lax.rem(c, count) == r // 2**level, 0.5**level, 0.0
        ).astype(bf16)

    def forward(part, load, size, valid, offset, unit):
        blocks_in = len(valid)
        step = size // blocks_in
        for pair in pairs_of(part):
            lanes = pair_lanes(pair)
            keys, values = load(0, lanes), load(1, lanes)
            outs = []
            for half in range(2):
                head = 2 * pair + half
                scores = dot_nt(keys, qm[head])
                blocks = [scores[i * step : (i + 1) * step] for i in range(blocks_in)]
                high = None
                for block, flag in zip(blocks, valid):
                    peak = jnp.max(block, axis=0, keepdims=True)
                    if flag is not None:
                        peak = jnp.where(flag, peak, -OUTSIDE)
                    high = peak if high is None else jnp.maximum(high, peak)
                weights, sums = [], None
                for block, flag in zip(blocks, valid):
                    shift = high if flag is None else jnp.where(flag, high, OUTSIDE)
                    weight = jnp.exp(block - shift)
                    added = jnp.sum(weight, axis=0, keepdims=True)
                    sums = added if sums is None else sums + added
                    weights.append(weight.astype(bf16))
                weight = weights[0] if blocks_in == 1 else jnp.concatenate(weights, axis=0)
                prob[head, offset : offset + size] = weight
                outs.append(dot_tn(weight, values))
                top[unit, head] = high
                total[unit, head] = sums
            out_part[unit, pair] = jnp.where(first_head, outs[0], outs[1])

    def near_load(slot):
        return lambda kv, lanes: near[slot, kv, :, lanes]

    def piece_load(level):
        return lambda kv, lanes: jnp.concatenate(
            [pieces[level - 1, slot, kv, :, lanes] for slot in range(3)], axis=0
        )

    far_valid = jnp.logical_or(
        jnp.logical_and(core == 0, me >= 1), jnp.logical_and(core == 1, me < n - 1)
    )
    level_valid = {}
    for level in range(1, LEVELS + 1):
        size = group_size(level)
        group, count = me // size, n // size
        odd = lax.rem(group, 2)
        third = group + 3 - 6 * odd
        level_valid[level] = [
            group >= 2,
            group + 2 < count,
            jnp.logical_and(third >= 0, third < count),
        ]

    def pass_on(part, level):
        lanes = group_lanes(part)
        for slot in range(3):
            at = 3 * (level - 1) + slot
            ref = pieces.at[level - 1, slot, :, half_rows, lanes]
            arrived(ref, plane_recv.at[part, at])
            remote(ref, ref, twin_send.at[part, at], twin_recv.at[part, at], twin)

    def pass_on_first(part):
        lanes = group_lanes(part)
        ref = pieces.at[0, core, :, :, lanes]
        arrived(ref, plane_recv.at[part, 0])
        remote(
            ref, pieces.at[0, 2, :, :, lanes],
            twin_send.at[part, 0], twin_recv.at[part, 0], twin,
        )

    def forward_level(part, level):
        lanes = group_lanes(part)
        if level == 1:
            arrived(pieces.at[0, 2, :, :, lanes], twin_recv.at[part, 0])
            arrived(pieces.at[0, 1 - core, :, :, lanes], twin_recv.at[part, 1])
        else:
            for slot in range(3):
                arrived(
                    pieces.at[level - 1, slot, :, other_rows, lanes],
                    twin_recv.at[part, 3 * (level - 1) + slot],
                )
        unit = NEAR_UNITS + level - 1
        forward(part, piece_load(level), 384, level_valid[level], unit_offset(unit), unit)

    def forward_own(part):
        forward(part, near_load(OWN), BLOCK, [None], unit_offset(0), 0)

    def forward_twin(part):
        arrived(near.at[twin_slot, :, :, group_lanes(part)], near_recv.at[part, 1])
        forward(part, near_load(twin_slot), BLOCK, [None], unit_offset(1), 1)

    def forward_far(part):
        lanes = group_lanes(part)
        arrived(near.at[far_slot, :, :, lanes], near_recv.at[part, 0])
        for kv in range(2):
            derived[kv, :, lanes] = dot_nn(average[...], near[far_slot, kv, :, lanes]).astype(bf16)
        remote(
            derived.at[:, :, lanes], pieces.at[0, core, :, :, lanes],
            twin_send.at[part, 1], twin_recv.at[part, 1], twin,
        )
        forward(part, near_load(far_slot), BLOCK, [far_valid], unit_offset(2), 2)

    units = range(NEAR_UNITS + LEVELS)
    head_row = lax.broadcasted_iota(jnp.int32, (8, 128), 0)
    head_lane = lax.broadcasted_iota(jnp.int32, (8, 128), 1) // 64
    head_sum = jnp.where(head_row == head_lane, 1.0, 0.0).astype(bf16)

    def finish(part):
        for pair in pairs_of(part):
            lanes = pair_lanes(pair)
            rows = []
            for half in range(2):
                head = 2 * pair + half
                high = functools.reduce(jnp.maximum, [top[unit, head] for unit in units])
                fades = [jnp.exp(top[unit, head] - high) for unit in units]
                scale = 1.0 / sum(fade * total[unit, head] for unit, fade in zip(units, fades))
                for unit, fade in zip(units, fades):
                    factor[unit, head] = fade * scale
                    rows.append(fade * scale)
            rows += [jnp.zeros_like(rows[0])] * (16 - len(rows))
            columns = jnp.transpose(jnp.concatenate(rows, axis=0))
            out = None
            for unit in units:
                second = len(units) + unit
                both = jnp.where(
                    first_head, columns[:, unit : unit + 1], columns[:, second : second + 1]
                )
                added = out_part[unit, pair] * both
                out = added if out is None else out + added
            att_ref[:, lanes] = out.astype(bf16)
            product = out * g_ref[:, lanes].astype(f32)
            coarse = product.astype(bf16)
            rest = (product - coarse.astype(f32)).astype(bf16)
            deltas = dot_nt(head_sum, coarse) + dot_nt(head_sum, rest)
            for half in range(2):
                delta[2 * pair + half] = deltas[half : half + 1]
                dq_part[2 * pair + half] = jnp.zeros((BLOCK, 128), f32)

    def backward(part, load, size, offset, unit, store):
        for pair in pairs_of(part):
            lanes = pair_lanes(pair)
            keys, values = load(0, lanes), load(1, lanes)
            key_part, value_part = None, None
            for half in range(2):
                head = 2 * pair + half
                wide = prob[head, offset : offset + size].astype(f32) * factor[unit, head]
                dscore = (wide * (dot_nt(values, gm[head]) - delta[head])).astype(bf16)
                key_new = dot_nn(dscore, qm[head])
                value_new = dot_nn(wide.astype(bf16), gm[head])
                key_part = key_new if key_part is None else key_part + key_new
                value_part = value_new if value_part is None else value_part + value_new
                dq_part[head] += dot_tn(dscore, keys)
            store(lanes, key_part, value_part)

    def near_store(slot):
        def store(lanes, key_part, value_part):
            near_grad[slot, 0, :, lanes] = key_part.astype(bf16)
            near_grad[slot, 1, :, lanes] = value_part.astype(bf16)
        return store

    def own_store(lanes, key_part, value_part):
        own_grad[0, :, lanes] = key_part
        own_grad[1, :, lanes] = value_part

    def piece_store(level):
        def store(lanes, key_part, value_part):
            for slot in range(3):
                at = slice(slot * 128, slot * 128 + 128)
                piece_grad[level - 1, slot, 0, :, lanes] = key_part[at].astype(bf16)
                piece_grad[level - 1, slot, 1, :, lanes] = value_part[at].astype(bf16)
        return store

    def backward_level(part, level):
        unit = NEAR_UNITS + level - 1
        backward(part, piece_load(level), 384, unit_offset(unit), unit, piece_store(level))
        lanes = group_lanes(part)
        if level == 1:
            for i, slot in enumerate((2, 1 - core)):
                remote(
                    piece_grad.at[0, slot, :, :, lanes], twin_first.at[i, :, :, lanes],
                    gtwin_send.at[part, i], gtwin_recv.at[part, i], twin,
                )
            return
        for slot in range(3):
            at = 3 * (level - 1) + slot
            remote(
                piece_grad.at[level - 1, slot, :, other_rows, lanes],
                twin_grad.at[level - 2, slot, :, :, lanes],
                gtwin_send.at[part, at], gtwin_recv.at[part, at], twin,
            )

    def grads_to_owners(part, level):
        lanes = group_lanes(part)
        rows = level_rows(level)
        for slot in range(3):
            arrived(
                twin_grad.at[level - 2, slot, :, :, lanes],
                gtwin_recv.at[part, 3 * (level - 1) + slot],
            )
            for kv in range(2):
                piece_grad[level - 1, slot, kv, half_rows, lanes] = (
                    piece_grad[level - 1, slot, kv, half_rows, lanes].astype(f32)
                    + twin_grad[level - 2, slot, kv, :, lanes].astype(f32)
                ).astype(bf16)
        targets = group_targets(level)
        place = {4: 1, 3: 4, 2: 10}[level]
        for slot in range(3):
            for chip in range(plane_chips(level)):
                if level == 4:
                    remote(
                        piece_grad.at[3, slot, :, half_rows, lanes],
                        row_grads.at[slot, :, :, lanes],
                        gplane_send.at[part, place], gplane_recv.at[part, 3 + slot],
                        plane_target(4, targets[slot], 0),
                    )
                else:
                    source = pl.multiple_of(core * 64 + chip * rows, 16)
                    base = contribution_base(level) + slot * 64
                    target = pl.multiple_of(base + chip_place(level) * rows, 16)
                    remote(
                        piece_grad.at[level - 1, slot, :, pl.ds(source, rows), lanes],
                        coarse_in.at[:, pl.ds(target, rows), lanes],
                        gplane_send.at[part, place], gplane_recv.at[part, level - 1],
                        plane_target(level, targets[slot], chip),
                    )
                place += 1

    def first_to_owner(part):
        lanes = group_lanes(part)
        arrived(twin_first.at[0, :, :, lanes], gtwin_recv.at[part, 0])
        for kv in range(2):
            piece_grad[0, core, kv, :, lanes] = (
                piece_grad[0, core, kv, :, lanes].astype(f32)
                + twin_first[0, kv, :, lanes].astype(f32)
            ).astype(bf16)
        remote(
            piece_grad.at[0, core, :, :, lanes], coarse_in.at[:, pl.ds(0, 128), lanes],
            gplane_send.at[part, 0], gplane_recv.at[part, 0], wrapped(me - 2 + 4 * core),
        )

    def backward_far(part):
        lanes = group_lanes(part)
        backward(part, near_load(far_slot), BLOCK, unit_offset(2), 2, near_store(1))
        arrived(twin_first.at[1, :, :, lanes], gtwin_recv.at[part, 1])
        for kv in range(2):
            near_grad[1, kv, :, lanes] = (
                near_grad[1, kv, :, lanes].astype(f32)
                + dot_nn(upsample[:, :128], twin_first[1, kv, :, lanes])
            ).astype(bf16)
        remote(
            near_grad.at[1, :, :, lanes], near_in.at[1, :, :, lanes],
            gnear_send.at[part, 1], gnear_recv.at[part, 1], far_device,
        )

    def backward_twin(part):
        lanes = group_lanes(part)
        backward(part, near_load(twin_slot), BLOCK, unit_offset(1), 1, near_store(0))
        remote(
            near_grad.at[0, :, :, lanes], near_in.at[0, :, :, lanes],
            gnear_send.at[part, 0], gnear_recv.at[part, 0], twin,
        )

    def backward_own(part):
        backward(part, near_load(OWN), BLOCK, unit_offset(0), 0, own_store)
        for pair in pairs_of(part):
            both = jnp.where(first_head, dq_part[2 * pair], dq_part[2 * pair + 1])
            dq_ref[:, pair_lanes(pair)] = (both * (1.0 / math.sqrt(HEAD))).astype(bf16)

    def row_to_owners(part):
        lanes = group_lanes(part)
        for slot in range(3):
            arrived(row_grads.at[slot, :, :, lanes], gplane_recv.at[part, 3 + slot])
        for kv in range(2):
            added = row_grads[0, kv, :, lanes].astype(f32) + row_grads[1, kv, :, lanes].astype(f32)
            row_sum[kv, :, lanes] = (added + row_grads[2, kv, :, lanes].astype(f32)).astype(bf16)
        target = pl.ds(pl.multiple_of(contribution_base(4) + row_place * 16, 16), 16)
        for kv in range(2):
            coarse_in[kv, target, lanes] = row_sum[kv, own_row, lanes]
        for step in (1, 3, 2):
            place, device = row_partner(step)
            remote(
                row_sum.at[:, pl.ds(pl.multiple_of(place * 16, 16), 16), lanes],
                coarse_in.at[:, target, lanes],
                grow_send.at[part, step - 1], grow_recv.at[part, step - 1], device,
            )

    def write(part):
        lanes = group_lanes(part)
        arrived(near_in.at[0, :, :, lanes], gnear_recv.at[part, 0])
        arrived(near_in.at[1, :, :, lanes], gnear_recv.at[part, 1])
        for level in range(1, LEVELS):
            base, width = contribution_base(level), contribution_width(level)
            arrived(coarse_in.at[:, pl.ds(base, width), lanes], gplane_recv.at[part, level - 1])
        for step in (1, 3, 2):
            base = contribution_base(4) + lax.rem(row_place + 4 - step, 4) * 16
            arrived(
                coarse_in.at[:, pl.ds(pl.multiple_of(base, 16), 16), lanes],
                grow_recv.at[part, step - 1],
            )
        for kv, out_ref in ((0, dk_ref), (1, dv_ref)):
            out = own_grad[kv, :, lanes] + near_in[0, kv, :, lanes].astype(f32)
            out = out + near_in[1, kv, :, lanes].astype(f32)
            out = out + dot_nn(upsample[...], coarse_in[kv, :, lanes])
            out_ref[:, lanes] = out.astype(bf16)

    forward_own(0)
    forward_own(1)
    forward_twin(0)
    pass_on(0, 3)
    pass_on(0, 2)
    forward_level(0, 3)
    pass_on(0, 4)
    pass_on_first(0)
    forward_level(0, 2)
    forward_far(0)
    forward_level(0, 4)
    forward_twin(1)
    forward_level(0, 1)
    finish(0)
    backward_level(0, 1)
    backward_level(0, 4)
    first_to_owner(0)
    backward_far(0)
    grads_to_owners(0, 4)
    backward_level(0, 3)
    backward_level(0, 2)
    grads_to_owners(0, 3)
    pass_on(1, 3)
    pass_on(1, 2)
    backward_twin(0)
    grads_to_owners(0, 2)
    pass_on(1, 4)
    pass_on_first(1)
    forward_level(1, 3)
    forward_level(1, 2)
    forward_level(1, 4)
    forward_far(1)
    backward_own(0)
    row_to_owners(0)
    forward_level(1, 1)
    finish(1)
    backward_level(1, 1)
    backward_level(1, 4)
    first_to_owner(1)
    backward_far(1)
    grads_to_owners(1, 4)
    backward_level(1, 3)
    backward_level(1, 2)
    grads_to_owners(1, 3)
    backward_twin(1)
    grads_to_owners(1, 2)
    row_to_owners(1)
    backward_own(1)
    write(0)
    write(1)
    for copy in started:
        copy.wait_send()


def hand_over(*refs):
    sources, targets, (held, in_sem, out_sem) = refs[:4], refs[4:8], refs[8:]
    inward = [
        pltpu.make_async_copy(source, held.at[i], in_sem.at[i]) for i, source in enumerate(sources)
    ]
    outward = [
        pltpu.make_async_copy(held.at[i], target, out_sem.at[i]) for i, target in enumerate(targets)
    ]
    for copy in inward:
        copy.start()
    for first, second in zip(inward, outward):
        first.wait()
        second.start()
    for copy in outward:
        copy.wait()


def on_device(device_count, sub_count, queries, keys, values, cotangent):
    vmem = pl.BlockSpec(memory_space=pltpu.VMEM)
    dma = pltpu.SemaphoreType.DMA
    rows = (BLOCK, FEATURES)
    plane_messages = 1 + 3 + 6 + 3
    scratch = [
        pltpu.VMEM((3, 2) + rows, bf16),
        pltpu.VMEM((2, 128, FEATURES), bf16),
        pltpu.VMEM((2, 64, FEATURES), bf16),
        pltpu.VMEM((2, 32, FEATURES), bf16),
        pltpu.VMEM((2, 16, FEATURES), bf16),
        pltpu.VMEM((LEVELS, 3, 2, 128, FEATURES), bf16),
        pltpu.VMEM((HEADS, BLOCK, 128), bf16),
        pltpu.VMEM((HEADS, BLOCK, 128), bf16),
        pltpu.VMEM((HEADS, KEYS, BLOCK), bf16),
        pltpu.VMEM((NEAR_UNITS + LEVELS, HEADS, 1, BLOCK), f32),
        pltpu.VMEM((NEAR_UNITS + LEVELS, HEADS, 1, BLOCK), f32),
        pltpu.VMEM((NEAR_UNITS + LEVELS, PAIRS, BLOCK, 128), f32),
        pltpu.VMEM((HEADS, BLOCK, 128), f32),
        pltpu.VMEM((NEAR_UNITS + LEVELS, HEADS, 1, BLOCK), f32),
        pltpu.VMEM((HEADS, 1, BLOCK), f32),
        pltpu.VMEM((BLOCK, CONTRIBUTIONS), bf16),
        pltpu.VMEM((128, BLOCK), bf16),
        pltpu.VMEM((2, 2) + rows, bf16),
        pltpu.VMEM((2,) + rows, f32),
        pltpu.VMEM((LEVELS, 3, 2, 128, FEATURES), bf16),
        pltpu.VMEM((LEVELS - 1, 3, 2, 64, FEATURES), bf16),
        pltpu.VMEM((2, 2, 128, FEATURES), bf16),
        pltpu.VMEM((2, 2) + rows, bf16),
        pltpu.VMEM((2, CONTRIBUTIONS, FEATURES), bf16),
        pltpu.VMEM((2, 64, FEATURES), bf16),
        pltpu.VMEM((3, 2, 64, FEATURES), bf16),
        pltpu.VMEM((2, 64, FEATURES), bf16),
        pltpu.VMEM((2, 128, FEATURES), bf16),
        dma((2, 2)), dma((2, 2)),
        dma((2, plane_messages)), dma((2, 3 * LEVELS)),
        dma((2, 3 * LEVELS)), dma((2, 3 * LEVELS)),
        dma((2, 2)), dma((2, 2)),
        dma((2, plane_messages)), dma((2, LEVELS + 2)),
        dma((2, 3 * LEVELS)), dma((2, 3 * LEVELS)),
        dma((3,)), dma((3,)), dma((2, 3)), dma((2, 3)),
    ]
    results = pl.pallas_call(
        functools.partial(kernel, device_count, sub_count),
        out_shape=[jax.ShapeDtypeStruct(rows, bf16)] * 4,
        in_specs=[vmem] * 4,
        out_specs=[vmem] * 4,
        scratch_shapes=scratch,
        compiler_params=pltpu.CompilerParams(
            collective_id=0, has_side_effects=True, vmem_limit_bytes=56 * 2**20
        ),
        name="hierarchical_attention",
    )(queries, keys, values, cotangent)
    anywhere = pl.BlockSpec(memory_space=pl.ANY)
    return pl.pallas_call(
        hand_over,
        out_shape=[jax.ShapeDtypeStruct(rows, bf16)] * 4,
        in_specs=[anywhere] * 4,
        out_specs=[anywhere] * 4,
        scratch_shapes=[pltpu.VMEM((4,) + rows, bf16), dma((4,)), dma((4,))],
        name="hand_over",
    )(*results)


def solution(mesh):
    spec = P(("seq", "sub"), None)
    device_count = mesh.shape["seq"] * mesh.shape["sub"]
    return jax.shard_map(
        functools.partial(on_device, device_count, mesh.shape["sub"]),
        mesh=mesh,
        in_specs=(spec,) * 4,
        out_specs=(spec,) * 4,
        check_vma=False,
    )
```
